512 devices in a mesh: seg: 32 (over z_lo, y), op: 16 (over x, z_hi, core).
Axes of the slice: x: 4, y: 8, z: 8 (z_hi: 2, z_lo: 4; z = z_hi * 4 + z_lo), core: 2. Of those that a mesh axis runs over, the one named last changes fastest.
Arguments:
- left_part: bfloat16 [32, 4, 256, 256], P('seg'), may hold values from -1 to 2
- right_part: bfloat16 [32, 4, 256, 256], P('seg'), may hold values from -1 to 2
- inverse_values: float32 [32, 4, 256], P('seg'), may hold values from 0.6 to 1.6
- left_env: bfloat16 [32, 48, 4, 256, 256], P('seg', 'op'), may hold values from -2 to 12
- right_env: bfloat16 [32, 48, 4, 256, 256], P('seg', 'op'), may hold values from -1 to 2
- source: int32 [48, 4], P('op'), may hold values from 0 to 3
- term_active: int32 [48], P('op'), may hold values from 0 to 1, as said below
- sketch: float32 [32, 256, 128], P('seg'), may hold values from -6 to 6
- kept: int32 [32, 4], P('seg'), may hold values from 32 to 128, as said below
Outputs:
- kept_state: bfloat16 [32, 4, 256, 256], P('seg')
- new_boundary: bfloat16 [32, 4, 128, 256], P('seg')
The draws below stay inside these ranges and needn't reach their ends.
Inputs may be any that keep to these rules, and one draw needn't show every extreme that they name: `kept`: in every junction one sector keeps exactly 128. `term_active`: on each index of op the filled slots come first and at least one is filled; on some index all 3 are, and on another exactly one is.
All inputs are finite; a program needn't handle non-finite values.
Results may differ from the reference program's by a relative error of at most 0.0093.
Values may be sent and summed in bfloat16 or wider, within the bound.
No kernel may reach another device: no remote copies, remote signals or barrier semaphores. Data moves between devices by JAX's collectives and lax.ppermute only.
A program may use at most 64 MiB of HBM per device.

```python
import math
import jax
import jax.numpy as jnp
from jax import lax

S = 256
NB = 4
KMAX = 128
W_DEV = 3
TERMS = 48
JUNCTIONS = 32


column_decay = 0.8


noise_level = 0.6


def grading(extent):
    steps = jnp.arange(extent, dtype=jnp.float32) / (extent - 1)
    return jnp.power(10.0, -column_decay * steps)


def near_identity(key, leading, extent):
    noise = jax.random.uniform(key, leading + (extent, extent), jnp.float32, -1.0, 1.0) * (noise_level / math.sqrt(extent))
    return noise + jnp.eye(extent, dtype=jnp.float32)


def draw_left_part(key, part):
    key = jax.random.fold_in(key, 5)
    return near_identity(key, (JUNCTIONS, NB), S).astype(jnp.bfloat16)


def draw_right_part(key, part):
    key = jax.random.fold_in(key, 7)
    blocks = near_identity(key, (JUNCTIONS, NB), S) * grading(S)[None, None, None, :]
    return blocks.astype(jnp.bfloat16)


def draw_left_env(key, part):
    key = jax.random.fold_in(key, 13)
    first_key, second_key = jax.random.split(key)
    scales = jnp.exp(jax.random.uniform(first_key, (JUNCTIONS, TERMS, NB, 1, 1), jnp.float32, math.log(0.1), math.log(10.0)))
    blocks = near_identity(second_key, (JUNCTIONS, TERMS, NB), S) * scales
    return blocks.astype(jnp.bfloat16)


def draw_right_env(key, part):
    key = jax.random.fold_in(key, 17)
    blocks = near_identity(key, (JUNCTIONS, TERMS, NB), S) * grading(S)[None, None, None, None, :]
    return blocks.astype(jnp.bfloat16)


def draw_source(key, part):
    key = jax.random.fold_in(key, 29)
    first_key, second_key = jax.random.split(key)
    own_sector = jnp.broadcast_to(jnp.arange(NB, dtype=jnp.int32)[None, :], (TERMS, NB))
    other_sector = (own_sector + jax.random.randint(first_key, (TERMS, NB), 1, NB)) % NB
    picks = jax.random.randint(second_key, (TERMS, NB), 0, 4)
    return jnp.where(picks == 0, other_sector, own_sector).astype(jnp.int32)


def draw_term_active(key, part):
    key = jax.random.fold_in(key, 11)
    first_key, second_key, third_key = jax.random.split(key, 3)
    shards = TERMS // W_DEV
    counts = jax.random.randint(first_key, (shards,), 1, W_DEV + 1)
    fullest = jax.random.randint(second_key, (), 0, shards)
    sparsest = (fullest + 1 + jax.random.randint(third_key, (), 0, shards - 1)) % shards
    places = jnp.arange(shards, dtype=jnp.int32)
    counts = jnp.where(places == fullest, W_DEV, counts)
    counts = jnp.where(places == sparsest, 1, counts)
    filled = jnp.arange(W_DEV, dtype=jnp.int32)[None, :] < counts[:, None]
    return filled.reshape(TERMS).astype(jnp.int32)


def draw_kept(key, part):
    key = jax.random.fold_in(key, 23)
    first_key, second_key = jax.random.split(key)
    counts = jax.random.randint(first_key, (JUNCTIONS, NB), KMAX // 4, KMAX + 1)
    widest = jax.random.randint(second_key, (JUNCTIONS,), 0, NB)
    counts = jnp.where(jnp.arange(NB, dtype=jnp.int32)[None, :] == widest[:, None], KMAX, counts)
    return counts.astype(jnp.int32)


def block_scale(stream_key, shape, pieces, least, top_value):
    loudness, own = 1.0, jax.random.fold_in(stream_key, 6)
    for position, shards_of in pieces:
        steps = jnp.exp(jax.random.uniform(jax.random.fold_in(own, position), (shards_of,), jnp.float32, least / len(pieces), top_value / len(pieces)))
        loudness = loudness * jnp.repeat(steps, shape[position] // shards_of).reshape([-1 if axis == position else 1 for axis in range(len(shape))])
    return loudness


def scatter_about(own_key, shape, scale, reach, cuts=(), held_as=jnp.bfloat16):
    gain = block_scale(own_key, shape, cuts, -0.22, 0.18) if cuts else 1.0
    result = jax.random.normal(own_key, shape, jnp.float32) * scale * gain
    return jnp.minimum(jnp.maximum(result, -reach), reach).astype(held_as)


def setup_inputs(seed: int = 0) -> dict:
    arg_keys = jax.random.split(jax.random.key(seed), 10)
    return {
        "left_part": draw_left_part(jax.random.fold_in(arg_keys[9], 71), 0),
        "right_part": draw_right_part(jax.random.fold_in(arg_keys[9], 71), 0),
        "inverse_values": jnp.clip(jnp.exp(math.log(1.6) - 0.98082923 * jax.random.uniform(arg_keys[2], (JUNCTIONS, NB, S), jnp.float32) ** block_scale(arg_keys[2], (JUNCTIONS, NB, S), ((0, 32),), -0.2, 0.2)), 0.6, 1.6),
        "left_env": draw_left_env(jax.random.fold_in(arg_keys[9], 71), 0),
        "right_env": draw_right_env(jax.random.fold_in(arg_keys[9], 71), 0),
        "source": draw_source(jax.random.fold_in(arg_keys[9], 71), 0),
        "term_active": draw_term_active(jax.random.fold_in(arg_keys[9], 71), 0),
        "sketch": scatter_about(arg_keys[7], (JUNCTIONS, S, KMAX), 1.0, 6.0, ((0, 32),), jnp.float32),
        "kept": draw_kept(jax.random.fold_in(arg_keys[9], 71), 0),
    }


def apply_terms(vector, left_env, right_env, source, active):
    start = jnp.zeros(vector.shape, jnp.float32)

    def add_term(total, packed):
        left_block, right_block, picks, flag = packed
        chosen = jnp.take(vector, picks, axis=0)
        inner = jnp.einsum('bij,bjk->bik', left_block.astype(jnp.float32), chosen.astype(jnp.float32)).astype(jnp.bfloat16)
        outer = jnp.einsum('bij,bjk->bik', inner.astype(jnp.float32), right_block.astype(jnp.float32))
        return (total + flag.astype(jnp.float32) * outer, None)
    total, unused = lax.scan(add_term, start, (left_env, right_env, source, active))
    return total

def solve_one(lower, correlation):
    return jax.scipy.linalg.cho_solve((lower, True), correlation)

def truncate(ground, sketch, kept):
    size = ground.shape[1]
    cols = sketch.shape[1]
    mask = (jnp.arange(cols, dtype=jnp.int32)[None, :] < kept[:, None]).astype(jnp.float32)
    basis = sketch[None] * mask[:, None, :]
    image = jnp.einsum('bij,bjk->bik', ground, basis, precision=lax.Precision.HIGHEST)
    gram = jnp.einsum('bik,bil->bkl', image, image, precision=lax.Precision.HIGHEST) / (size * size)
    gram = gram + jnp.eye(cols, dtype=jnp.float32)[None] * (1.0 - mask)[:, None, :]
    lower = jnp.linalg.cholesky(gram)
    correlation = jnp.einsum('bik,bij->bkj', image, ground, precision=lax.Precision.HIGHEST)
    right = jax.vmap(solve_one)(lower, correlation) / size
    state = jnp.einsum('bik,bkj->bij', image, right, precision=lax.Precision.HIGHEST) / size
    return (state.astype(jnp.bfloat16), right.astype(jnp.bfloat16))

def reference(left_part, right_part, inverse_values, left_env, right_env, source, term_active, sketch, kept):
    neighbours = jnp.roll(right_part, -1, axis=0)

    def junction(packed):
        own_left, neighbour, values, lenv, renv, test_matrix, kept_counts = packed
        scaled = (own_left.astype(jnp.float32) * values[:, None, :]).astype(jnp.bfloat16)
        center = jnp.einsum('bij,bjk->bik', scaled.astype(jnp.float32), neighbour.astype(jnp.float32))
        first_vec = center / jnp.sqrt(jnp.mean(center * center) + 1e-06)
        first_img = apply_terms(first_vec.astype(jnp.bfloat16), lenv, renv, source, term_active)
        ray_first = jnp.mean(first_vec * first_img)
        resid = first_img - ray_first * first_vec
        coupling = jnp.sqrt(jnp.mean(resid * resid) + 1e-06)
        second_vec = resid / coupling
        second_img = apply_terms(second_vec.astype(jnp.bfloat16), lenv, renv, source, term_active)
        ray_second = jnp.mean(second_vec * second_img)
        lowest = 0.5 * (ray_first + ray_second) - jnp.sqrt(0.25 * (ray_second - ray_first) ** 2 + coupling ** 2)
        weight = ray_second - lowest
        length = jnp.sqrt(weight ** 2 + coupling ** 2)
        ground = (weight * first_vec - coupling * second_vec) / length
        return truncate(ground, test_matrix, kept_counts)
    kept_state, right_factor = lax.map(junction, (left_part, neighbours, inverse_values, left_env, right_env, sketch, kept))
    return (kept_state, jnp.roll(right_factor, 1, axis=0))
```

```python
import jax
import jax.numpy as jnp
from jax import lax
from jax.sharding import PartitionSpec as P


def from_behind(array, axis, by):
    size = lax.axis_size(axis)
    return lax.ppermute(array, axis, [(i, (i + by) % size) for i in range(size)])


def plane_groups():
    return [[x * 4 + z * 2 + c for x in range(4) for c in range(2)] for z in range(2)]


def apply_terms(vector, left_env, right_env, source, active):
    total = jnp.zeros(vector.shape, jnp.float32)

    def keep_total(current):
        return current

    for slot_number in range(left_env.shape[0]):

        def add_term(current, slot_number=slot_number):
            chosen = jnp.take(vector, source[slot_number], axis=0)
            inner = jnp.einsum(
                "bij,bjk->bik", left_env[slot_number], chosen, preferred_element_type=jnp.float32
            ).astype(jnp.bfloat16)
            return current + jnp.einsum(
                "bij,bjk->bik", inner, right_env[slot_number], preferred_element_type=jnp.float32
            )

        total = lax.cond(active[slot_number] > 0, add_term, keep_total, total)
    return total


def solve_one(lower, correlation):
    return jax.scipy.linalg.cho_solve((lower, True), correlation)


def truncate(ground, sketch, kept):
    size = ground.shape[1]
    cols = sketch.shape[1]
    mask = (jnp.arange(cols, dtype=jnp.int32)[None, :] < kept[:, None]).astype(jnp.float32)
    basis = sketch[None] * mask[:, None, :]
    image = jnp.einsum("bij,bjk->bik", ground, basis, precision=lax.Precision.HIGHEST)
    gram = jnp.einsum("bik,bil->bkl", image, image, precision=lax.Precision.HIGHEST) / (size * size)
    gram = gram + jnp.eye(cols, dtype=jnp.float32)[None] * (1.0 - mask)[:, None, :]
    lower = jnp.linalg.cholesky(gram)
    correlation = jnp.einsum("bik,bij->bkj", image, ground, precision=lax.Precision.HIGHEST)
    right = jax.vmap(solve_one)(lower, correlation) / size
    state = jnp.einsum("bik,bkj->bij", image, right, precision=lax.Precision.HIGHEST) / size
    return (state.astype(jnp.bfloat16), right.astype(jnp.bfloat16))


def lowest_ritz(first_vec, second_vec, ray_first, ray_second, coupling):
    lowest = 0.5 * (ray_first + ray_second) - jnp.sqrt(
        0.25 * (ray_second - ray_first) ** 2 + coupling**2
    )
    weight = ray_second - lowest
    length = jnp.sqrt(weight**2 + coupling**2)
    return (weight * first_vec - coupling * second_vec) / length


def sum_over_op(part):
    chunks = part.astype(jnp.bfloat16).reshape(8, 128, 256)
    chunks = lax.all_to_all(chunks, "op", 0, 0, axis_index_groups=plane_groups(), tiled=True)
    own = jnp.sum(chunks.astype(jnp.float32), axis=0).astype(jnp.bfloat16)
    other = lax.ppermute(own, "op", [(i, i ^ 2) for i in range(16)])
    both = (own.astype(jnp.float32) + other.astype(jnp.float32)).astype(jnp.bfloat16)
    spread = jnp.broadcast_to(both[None], (8, 128, 256))
    whole = lax.all_to_all(spread, "op", 0, 0, axis_index_groups=plane_groups(), tiled=True)
    return whole.reshape(4, 256, 256).astype(jnp.float32)


def shards(
    left_part, right_part, inverse_values, left_env, right_env, source, term_active, sketch, kept
):
    neighbour = from_behind(right_part, "seg", -1)
    scaled = (left_part[0].astype(jnp.float32) * inverse_values[0][:, None, :]).astype(jnp.bfloat16)
    center = jnp.einsum("bij,bjk->bik", scaled, neighbour[0], preferred_element_type=jnp.float32)
    first_vec = center / jnp.sqrt(jnp.mean(center * center) + 1e-06)
    lenv = left_env[0]
    renv = right_env[0]

    def product(vector):
        return apply_terms(vector, lenv, renv, source, term_active)

    first_part = product(first_vec.astype(jnp.bfloat16))
    ray_part = jnp.mean(first_vec * first_part)
    resid = sum_over_op(first_part - ray_part * first_vec)
    coupling = jnp.sqrt(jnp.mean(resid * resid) + 1e-06)
    second_vec = resid / coupling
    second_part = product(second_vec.astype(jnp.bfloat16))
    rays = jnp.stack([ray_part, jnp.mean(second_vec * second_part)])
    rays = jnp.broadcast_to(jnp.pad(rays, (0, 126))[None], (16, 128))
    rays = jnp.sum(lax.all_to_all(rays, "op", 0, 0, tiled=True), axis=0)
    ground = lowest_ritz(first_vec, second_vec, rays[0], rays[1], coupling)
    kept_state, right_factor = truncate(ground, sketch[0], kept[0])
    handed = from_behind(right_factor, "seg", 1)
    return (kept_state[None], handed[None])


def solution(mesh):
    placed = (
        P("seg", None, None, None),
        P("seg", None, None, None),
        P("seg", None, None),
        P("seg", "op", None, None, None),
        P("seg", "op", None, None, None),
        P("op", None),
        P("op"),
        P("seg", None, None),
        P("seg", None),
    )
    return jax.shard_map(
        shards,
        mesh=mesh,
        in_specs=placed,
        out_specs=(P("seg", None, None, None), P("seg", None, None, None)),
        check_vma=False,
    )
```

```python
import jax
import jax.numpy as jnp
from jax import lax
from jax.experimental import pallas as pl
from jax.experimental.pallas import tpu as pltpu
from jax.sharding import PartitionSpec as P

bf16, f32 = jnp.bfloat16, jnp.float32


def env_copies(lenv_hbm, renv_hbm, lenv, renv, sems):
    copies = []
    for slot in range(lenv_hbm.shape[0]):
        copies.append(pltpu.make_async_copy(lenv_hbm.at[slot], lenv.at[slot], sems.at[slot, 0]))
        copies.append(
            pltpu.make_async_copy(
                renv_hbm.at[slot], renv.at[:, pl.ds(slot * 256, 256), :], sems.at[slot, 1]
            )
        )
    return copies


def own_terms(source, active, vector, lenv, renv, inner, copies, image):
    slots, sectors = lenv.shape[0], lenv.shape[1]
    for slot in range(slots):
        copies[2 * slot].wait()
        flag = active[slot].astype(f32)
        for b in range(sectors):
            product = jnp.dot(
                lenv[slot, b], vector[source[slot, b]], preferred_element_type=f32
            )
            inner[b, :, slot * 256 : (slot + 1) * 256] = (product * flag).astype(bf16)
    for slot in range(slots):
        copies[2 * slot + 1].wait()
    for b in range(sectors):
        image[b] = jnp.dot(inner[b], renv[b], preferred_element_type=f32)


def first_kernel(
    source, active, left_part, inverse, neighbour, lenv_hbm, renv_hbm,
    first, part, ray, lenv, renv, inner, vector, image, sems,
):
    copies = env_copies(lenv_hbm, renv_hbm, lenv, renv, sems)
    for copy in copies:
        copy.start()
    sectors = left_part.shape[0]
    count = sectors * 256 * 256
    squares = jnp.zeros((1, 256), f32)
    for b in range(sectors):
        scaled = (left_part[b].astype(f32) * inverse[b : b + 1, :]).astype(bf16)
        center = jnp.dot(scaled, neighbour[b], preferred_element_type=f32)
        first[b] = center
        squares += jnp.sum(center * center, axis=0, keepdims=True)
    scale = lax.rsqrt(jnp.sum(squares, axis=1, keepdims=True) / count + 1e-06)
    for b in range(sectors):
        scaled_center = first[b] * scale
        first[b] = scaled_center
        vector[b] = scaled_center.astype(bf16)
    own_terms(source, active, vector, lenv, renv, inner, copies, image)
    dots = jnp.zeros((1, 256), f32)
    for b in range(sectors):
        dots += jnp.sum(first[b] * image[b], axis=0, keepdims=True)
    own_ray = jnp.sum(dots, axis=1, keepdims=True) / count
    for b in range(sectors):
        part[b] = (image[b] - own_ray * first[b]).astype(bf16)
    ray[...] = jnp.broadcast_to(own_ray, ray.shape)


def second_kernel(
    source, active, resid, first_ray, lenv_hbm, renv_hbm,
    rays, coupling, lenv, renv, inner, vector, image, sems,
):
    copies = env_copies(lenv_hbm, renv_hbm, lenv, renv, sems)
    for copy in copies:
        copy.start()
    sectors = resid.shape[0]
    count = sectors * 256 * 256
    squares = jnp.zeros((1, 256), f32)
    for b in range(sectors):
        piece = resid[b].astype(f32)
        squares += jnp.sum(piece * piece, axis=0, keepdims=True)
    mean_square = jnp.sum(squares, axis=1, keepdims=True) / count + 1e-06
    scale = lax.rsqrt(mean_square)
    for b in range(sectors):
        vector[b] = (resid[b].astype(f32) * scale).astype(bf16)
    own_terms(source, active, vector, lenv, renv, inner, copies, image)
    dots = jnp.zeros((1, 256), f32)
    for b in range(sectors):
        dots += jnp.sum(resid[b].astype(f32) * image[b], axis=0, keepdims=True)
    own_ray = jnp.sum(dots, axis=1, keepdims=True) * scale / count
    lane = lax.broadcasted_iota(jnp.int32, rays.shape, 1)
    rays[...] = jnp.where(lane == 0, first_ray[0:1, :], jnp.broadcast_to(own_ray, rays.shape))
    coupling[...] = jnp.broadcast_to(jnp.sqrt(mean_square), coupling.shape)


SMEM = pl.BlockSpec(memory_space=pltpu.SMEM)
VMEM = pl.BlockSpec(memory_space=pltpu.VMEM)
ANY = pl.BlockSpec(memory_space=pl.ANY)


def env_scratch(slots, sectors):
    return [
        pltpu.VMEM((slots, sectors, 256, 256), bf16),
        pltpu.VMEM((sectors, slots * 256, 256), bf16),
        pltpu.VMEM((sectors, 256, slots * 256), bf16),
        pltpu.VMEM((sectors, 256, 256), bf16),
        pltpu.VMEM((sectors, 256, 256), f32),
        pltpu.SemaphoreType.DMA((slots, 2)),
    ]


def first_step(source, active, left_part, inverse, neighbour, lenv, renv):
    slots, sectors = lenv.shape[:2]
    return pl.pallas_call(
        first_kernel,
        out_shape=(
            jax.ShapeDtypeStruct((sectors, 256, 256), f32),
            jax.ShapeDtypeStruct((sectors, 256, 256), bf16),
            jax.ShapeDtypeStruct((8, 128), f32),
        ),
        in_specs=[SMEM, SMEM, VMEM, VMEM, VMEM, ANY, ANY],
        out_specs=(VMEM, VMEM, VMEM),
        scratch_shapes=env_scratch(slots, sectors),
        compiler_params=pltpu.CompilerParams(vmem_limit_bytes=24 * 2**20),
        cost_estimate=pl.CostEstimate(flops=940_000_000, bytes_accessed=6_000_000, transcendentals=0),
    )(source, active, left_part, inverse, neighbour, lenv, renv)


def second_step(source, active, resid, first_ray, lenv, renv):
    slots, sectors = lenv.shape[:2]
    return pl.pallas_call(
        second_kernel,
        out_shape=(
            jax.ShapeDtypeStruct((16, 128), f32),
            jax.ShapeDtypeStruct((8, 128), f32),
        ),
        in_specs=[SMEM, SMEM, VMEM, VMEM, ANY, ANY],
        out_specs=(VMEM, VMEM),
        scratch_shapes=env_scratch(slots, sectors),
        compiler_params=pltpu.CompilerParams(vmem_limit_bytes=24 * 2**20),
        cost_estimate=pl.CostEstimate(flops=800_000_000, bytes_accessed=4_000_000, transcendentals=0),
    )(source, active, resid, first_ray, lenv, renv)


HIGHEST = lax.Precision.HIGHEST
NN = (((1,), (0,)), ((), ()))
NT = (((1,), (1,)), ((), ()))
TN = (((0,), (0,)), ((), ()))


def exact_dot(left, right, dims=NN):
    return lax.dot_general(left, right, dims, precision=HIGHEST, preferred_element_type=f32)


def split(array):
    high = array.astype(bf16)
    return high, (array - high.astype(f32)).astype(bf16)


def fine_dot(left, right, dims=NN):
    def dot(a, b):
        return lax.dot_general(a, b, dims, preferred_element_type=f32)
    return dot(left[0], right[0]) + (dot(left[0], right[1]) + dot(left[1], right[0]))


def invert_blocks(packed):
    size = packed.shape[0]
    row = lax.broadcasted_iota(jnp.int32, packed.shape, 0)
    lane = lax.broadcasted_iota(jnp.int32, packed.shape, 1)
    place = lane % size
    start = lane - place

    def column(array, k):
        return jnp.take_along_axis(array, start + k, axis=1)

    here = column(packed, 0)
    for k in range(size):
        ahead = column(packed, k + 1) if k + 1 < size else None
        inverse = 1.0 / here[k : k + 1, :]
        pivot_row = jnp.where(place[k : k + 1, :] == k, 1.0, packed[k : k + 1, :]) * inverse
        packed = jnp.where(place == k, 0.0, packed) - here * pivot_row
        packed = jnp.where(row == k, pivot_row, packed)
        if ahead is not None:
            factor = here[k + 1 : k + 2, :] * inverse
            here = jnp.where(row == k, factor, ahead - here * factor)
    return packed


def invert(gram):
    sectors, cols, size = len(gram), gram[0].shape[0], 32
    row = lax.broadcasted_iota(jnp.int32, (cols, cols), 0)
    lane = lax.broadcasted_iota(jnp.int32, (cols, cols), 1)
    same = (row // size) == (lane // size)
    unit = jnp.where(row % size == lane % size, 1.0, 0.0).astype(f32)
    block_lane = lax.broadcasted_iota(jnp.int32, (size, cols), 1) // size
    for p in range(cols // size):
        rows = slice(p * size, (p + 1) * size)
        packed = jnp.zeros((size, cols), f32)
        for s in range(sectors):
            turned = pltpu.roll(gram[s][rows], ((s - p) * size) % cols, 1) if s != p else gram[s][rows]
            packed = jnp.where(block_lane == s, turned, packed)
        inverse = invert_blocks(packed)
        inverse = jnp.where(same, jnp.concatenate([inverse] * sectors, axis=0), 0.0)
        stacked = jnp.concatenate([g[rows] for g in gram], axis=0)
        stacked = jnp.where(lane // size == p, unit, stacked)
        panel = exact_dot(inverse, stacked)
        for s in range(sectors):
            own = panel[s * size : (s + 1) * size]
            tiled = jnp.concatenate([own] * (cols // size), axis=0)
            factor = jnp.where((lane // size == p) & (row // size != p), gram[s], 0.0)
            rest = jnp.where(lane // size == p, 0.0, gram[s])
            rest = jnp.where(row // size == p, tiled, rest)
            gram[s] = rest - exact_dot(factor, tiled)
    return gram


def truncate_kernel(kept, rays, coupling, first, resid, sketch, right, right_low, image):
    sectors, size = first.shape[:2]
    cols = sketch.shape[0]
    sums = jnp.sum(rays[...], axis=0, keepdims=True)
    ray_first, ray_second = sums[:, 0:1], sums[:, 1:2]
    between = coupling[0:1, 0:1]
    half = 0.5 * (ray_second - ray_first)
    weight = half + jnp.sqrt(half * half + between * between)
    length = lax.rsqrt(weight * weight + between * between)
    of_first, of_resid = weight * length, length
    tests = split(sketch[...])
    row = lax.broadcasted_iota(jnp.int32, (cols, cols), 0)
    lane = lax.broadcasted_iota(jnp.int32, (cols, cols), 1)
    gram, correlation = [], []
    for b in range(sectors):
        ground = split(of_first * first[b] - of_resid * resid[b].astype(f32))
        wide = lax.broadcasted_iota(jnp.int32, (cols, size), 0) < kept[0, b]
        own = jnp.where(wide, fine_dot(tests, ground, NT), 0.0)
        image[b] = own
        own = split(own)
        empty = jnp.where((row == lane) & (row >= kept[0, b]), 1.0, 0.0)
        gram.append(fine_dot(own, own, NT) * (1.0 / (size * size)) + empty)
        correlation.append(fine_dot(own, ground))
    gram = invert(gram)
    for b in range(sectors):
        own = exact_dot(gram[b], correlation[b]) * (1.0 / size)
        right[b] = own
        right_low[b] = own.astype(bf16)


def truncate_step(kept, rays, coupling, first, resid, sketch):
    sectors, size = first.shape[:2]
    cols = sketch.shape[0]
    return pl.pallas_call(
        truncate_kernel,
        out_shape=(
            jax.ShapeDtypeStruct((sectors, cols, size), f32),
            jax.ShapeDtypeStruct((sectors, cols, size), bf16),
            jax.ShapeDtypeStruct((sectors, cols, size), f32),
        ),
        in_specs=[SMEM] + [VMEM] * 5,
        out_specs=(VMEM, VMEM, VMEM),
        compiler_params=pltpu.CompilerParams(vmem_limit_bytes=24 * 2**20),
        cost_estimate=pl.CostEstimate(flops=900_000_000, bytes_accessed=4_000_000, transcendentals=0),
    )(kept, rays, coupling, first, resid, sketch)


def from_behind(array, axis, by):
    size = lax.axis_size(axis)
    return lax.ppermute(array, axis, [(i, (i + by) % size) for i in range(size)])


def plane_groups():
    return [[x * 4 + z * 2 + c for x in range(4) for c in range(2)] for z in range(2)]


def sum_over_op(part):
    chunks = part.reshape(8, 128, 256)
    chunks = lax.all_to_all(chunks, "op", 0, 0, axis_index_groups=plane_groups(), tiled=True)
    own = jnp.sum(chunks.astype(f32), axis=0).astype(bf16)
    other = lax.ppermute(own, "op", [(i, i ^ 2) for i in range(16)])
    both = (own.astype(f32) + other.astype(f32)).astype(bf16)
    spread = jnp.broadcast_to(both[None], (8, 128, 256))
    whole = lax.all_to_all(spread, "op", 0, 0, axis_index_groups=plane_groups(), tiled=True)
    return whole.reshape(4, 256, 256)


def shards(
    left_part, right_part, inverse_values, left_env, right_env, source, term_active, sketch, kept
):
    neighbour = from_behind(right_part, "seg", -1)
    lenv, renv = left_env[0], right_env[0]
    tests = sketch[0].T
    first, part, ray = first_step(
        source, term_active, left_part[0], inverse_values[0], neighbour[0], lenv, renv
    )
    resid = sum_over_op(part)
    rays, coupling = second_step(source, term_active, resid, ray, lenv, renv)
    rays = lax.all_to_all(rays, "op", 0, 0, tiled=True)
    right, right_low, image = truncate_step(kept, rays, coupling, first, resid, tests)
    handed = from_behind(right_low, "seg", 1)
    kept_state = jnp.einsum("bki,bkj->bij", image, right, precision=HIGHEST) / 256
    return (kept_state.astype(bf16)[None], handed[None])


def solution(mesh):
    placed = (
        P("seg", None, None, None),
        P("seg", None, None, None),
        P("seg", None, None),
        P("seg", "op", None, None, None),
        P("seg", "op", None, None, None),
        P("op", None),
        P("op"),
        P("seg", None, None),
        P("seg", None),
    )
    return jax.shard_map(
        shards,
        mesh=mesh,
        in_specs=placed,
        out_specs=(P("seg", None, None, None), P("seg", None, None, None)),
        check_vma=False,
    )
```

```python
import jax
import jax.numpy as jnp
from jax import lax
from jax.experimental import pallas as pl
from jax.experimental.pallas import tpu as pltpu
from jax.sharding import PartitionSpec as P

bf16, f32 = jnp.bfloat16, jnp.float32
HIGHEST = lax.Precision.HIGHEST
NN = (((1,), (0,)), ((), ()))
NT = (((1,), (1,)), ((), ()))

SMEM = pl.BlockSpec(memory_space=pltpu.SMEM)
VMEM = pl.BlockSpec(memory_space=pltpu.VMEM)
HBM = pl.BlockSpec(memory_space=pltpu.HBM)


def call(kernel, operands, in_specs, outs, out_specs, scratch=(), flops=0, moved=0):
    return pl.pallas_call(
        kernel,
        out_shape=tuple(jax.ShapeDtypeStruct(shape, dtype) for shape, dtype in outs),
        in_specs=in_specs,
        out_specs=tuple(out_specs),
        scratch_shapes=list(scratch),
        compiler_params=pltpu.CompilerParams(vmem_limit_bytes=24 * 2**20),
        cost_estimate=pl.CostEstimate(flops=flops, bytes_accessed=moved, transcendentals=0),
    )(*operands)


def prepare_kernel(left_part, inverse, lenv_hbm, renv_hbm, scaled, lenv, renv, sems):
    copies = []
    for slot in range(lenv.shape[0]):
        rows = pl.ds(slot * 256, 256)
        copies.append(pltpu.make_async_copy(lenv_hbm.at[slot], lenv.at[slot], sems.at[slot, 0]))
        copies.append(
            pltpu.make_async_copy(renv_hbm.at[slot], renv.at[:, rows, :], sems.at[slot, 1])
        )
    for copy in copies:
        copy.start()
    for b in range(left_part.shape[0]):
        scaled[b] = (left_part[b].astype(f32) * inverse[b : b + 1, :]).astype(bf16)
    for copy in copies:
        copy.wait()


def first_kernel(
    source, active, scaled, neighbour, lenv, renv,
    first_hbm, part, ray, first, inner, vector, image, sems,
):
    slots, sectors = lenv.shape[:2]
    count = sectors * 256 * 256
    squares = jnp.zeros((1, 256), f32)
    for b in range(sectors):
        center = jnp.dot(scaled[b], neighbour[b], preferred_element_type=f32)
        image[b] = center
        squares += jnp.sum(center * center, axis=0, keepdims=True)
    scale = lax.rsqrt(jnp.sum(squares, axis=1, keepdims=True) / count + 1e-06)
    out_copies = []
    for b in range(sectors):
        scaled_center = image[b] * scale
        first[b] = scaled_center
        out_copies.append(pltpu.make_async_copy(first.at[b], first_hbm.at[b], sems.at[b]))
        out_copies[b].start()
        vector[b] = scaled_center.astype(bf16)
    for slot in range(slots):
        flag = active[slot].astype(f32)
        for b in range(sectors):
            product = jnp.dot(
                lenv[slot, b], vector[source[slot, b]], preferred_element_type=f32
            )
            inner[b, :, slot * 256 : (slot + 1) * 256] = (product * flag).astype(bf16)
    dots = jnp.zeros((1, 256), f32)
    for b in range(sectors):
        own = jnp.dot(inner[b], renv[b], preferred_element_type=f32)
        image[b] = own
        dots += jnp.sum(first[b] * own, axis=0, keepdims=True)
    own_ray = jnp.sum(dots, axis=1, keepdims=True) / count
    for b in range(sectors):
        part[b] = (image[b] - own_ray * first[b]).astype(bf16)
    ray[...] = jnp.broadcast_to(own_ray, ray.shape)
    for copy in out_copies:
        copy.wait()


def second_kernel(source, active, resid, first_ray, lenv, renv, rays, coupling, inner, vector):
    slots, sectors = lenv.shape[:2]
    count = sectors * 256 * 256
    squares = jnp.zeros((1, 256), f32)
    for b in range(sectors):
        piece = resid[b].astype(f32)
        squares += jnp.sum(piece * piece, axis=0, keepdims=True)
    mean_square = jnp.sum(squares, axis=1, keepdims=True) / count + 1e-06
    scale = lax.rsqrt(mean_square)
    for b in range(sectors):
        vector[b] = (resid[b].astype(f32) * scale).astype(bf16)
    for slot in range(slots):
        flag = active[slot].astype(f32)
        for b in range(sectors):
            product = jnp.dot(
                lenv[slot, b], vector[source[slot, b]], preferred_element_type=f32
            )
            inner[b, :, slot * 256 : (slot + 1) * 256] = (product * flag).astype(bf16)
    dots = jnp.zeros((1, 256), f32)
    for b in range(sectors):
        own = jnp.dot(inner[b, :, :256], renv[0, b], preferred_element_type=f32)
        for slot in range(1, slots):
            lanes = slice(slot * 256, (slot + 1) * 256)
            own += jnp.dot(inner[b, :, lanes], renv[slot, b], preferred_element_type=f32)
        dots += jnp.sum(resid[b].astype(f32) * own, axis=0, keepdims=True)
    own_ray = jnp.sum(dots, axis=1, keepdims=True) * scale / count
    lane = lax.broadcasted_iota(jnp.int32, rays.shape, 1)
    rays[...] = jnp.where(lane == 0, first_ray[0:1, :], jnp.broadcast_to(own_ray, rays.shape))
    coupling[...] = jnp.broadcast_to(jnp.sqrt(mean_square), coupling.shape)


def split(array):
    high = array.astype(bf16)
    return high, (array - high.astype(f32)).astype(bf16)


def dot(left, right, dims=NN):
    return lax.dot_general(left, right, dims, preferred_element_type=f32)


def fine_dot(left, right, dims=NN):
    return dot(left[0], right[0], dims) + (
        dot(left[0], right[1], dims) + dot(left[1], right[0], dims)
    )


def exact_dot(left, right, dims=NN):
    return lax.dot_general(left, right, dims, precision=HIGHEST, preferred_element_type=f32)


def quadratic_kernel(kept, first, resid, sketch, images, grams, corr_ff, corr_x, corr_ss):
    sectors, size = first.shape[:2]
    cols = sketch.shape[0]
    tests = split(sketch[...])
    row = lax.broadcasted_iota(jnp.int32, (cols, size), 0)
    for b in range(sectors):
        wide = row < kept[0, b]
        other = resid[b]
        ground = split(first[b])
        of_first = jnp.where(wide, fine_dot(tests, ground, NT), 0.0)
        of_resid = jnp.where(wide, dot(tests[0], other, NT) + dot(tests[1], other, NT), 0.0)
        images[b, :cols] = of_first
        images[b, cols:] = of_resid
        both = split(images[b])
        grams[b] = fine_dot(both, both, NT)
        with_first = fine_dot(both, ground)
        with_resid = dot(both[0], other) + dot(both[1], other)
        corr_ff[b] = with_first[:cols]
        corr_x[b] = with_first[cols:] + with_resid[:cols]
        corr_ss[b] = with_resid[cols:]


def invert_blocks(packed):
    size = packed.shape[0]
    row = lax.broadcasted_iota(jnp.int32, packed.shape, 0)
    lane = lax.broadcasted_iota(jnp.int32, packed.shape, 1)
    place = lane % size
    start = lane - place

    def column(array, k):
        return jnp.take_along_axis(array, start + k, axis=1)

    here = column(packed, 0)
    for k in range(size):
        ahead = column(packed, k + 1) if k + 1 < size else None
        inverse = 1.0 / here[k : k + 1, :]
        pivot_row = jnp.where(place[k : k + 1, :] == k, 1.0, packed[k : k + 1, :]) * inverse
        packed = jnp.where(place == k, 0.0, packed) - here * pivot_row
        packed = jnp.where(row == k, pivot_row, packed)
        if ahead is not None:
            factor = here[k + 1 : k + 2, :] * inverse
            here = jnp.where(row == k, factor, ahead - here * factor)
    return packed


def invert(gram):
    sectors, cols, size = len(gram), gram[0].shape[0], 32
    row = lax.broadcasted_iota(jnp.int32, (cols, cols), 0)
    lane = lax.broadcasted_iota(jnp.int32, (cols, cols), 1)
    same = (row // size) == (lane // size)
    unit = jnp.where(row % size == lane % size, 1.0, 0.0).astype(f32)
    block_lane = lax.broadcasted_iota(jnp.int32, (size, cols), 1) // size
    for p in range(cols // size):
        rows = slice(p * size, (p + 1) * size)
        packed = jnp.zeros((size, cols), f32)
        for s in range(sectors):
            shift = ((s - p) * size) % cols
            turned = pltpu.roll(gram[s][rows], shift, 1) if shift else gram[s][rows]
            packed = jnp.where(block_lane == s, turned, packed)
        inverse = invert_blocks(packed)
        inverse = jnp.where(same, jnp.concatenate([inverse] * sectors, axis=0), 0.0)
        stacked = jnp.concatenate([g[rows] for g in gram], axis=0)
        stacked = jnp.where(lane // size == p, unit, stacked)
        panel = exact_dot(inverse, stacked)
        for s in range(sectors):
            own = panel[s * size : (s + 1) * size]
            tiled = jnp.concatenate([own] * (cols // size), axis=0)
            factor = jnp.where((lane // size == p) & (row // size != p), gram[s], 0.0)
            rest = jnp.where(lane // size == p, 0.0, gram[s])
            rest = jnp.where(row // size == p, tiled, rest)
            gram[s] = rest - exact_dot(factor, tiled)
    return gram


def solve_kernel(
    kept, rays, coupling, images, grams, corr_ff, corr_x, corr_ss, right, right_low, image
):
    sectors, size = corr_x.shape[0], corr_x.shape[2]
    cols = corr_x.shape[1]
    sums = jnp.sum(rays[...], axis=0, keepdims=True)
    ray_first, ray_second = sums[:, 0:1], sums[:, 1:2]
    between = coupling[0:1, 0:1]
    half = 0.5 * (ray_second - ray_first)
    weight = half + jnp.sqrt(half * half + between * between)
    length = lax.rsqrt(weight * weight + between * between)
    of_first, of_resid = weight * length, -length
    ff, fs, ss = of_first * of_first, of_first * of_resid, of_resid * of_resid
    row = lax.broadcasted_iota(jnp.int32, (cols, cols), 0)
    lane = lax.broadcasted_iota(jnp.int32, (cols, cols), 1)
    gram = []
    for b in range(sectors):
        empty = jnp.where((row == lane) & (row >= kept[0, b]), 1.0, 0.0)
        mixed = grams[b, :cols, cols:] + grams[b, cols:, :cols]
        own = ff * grams[b, :cols, :cols] + fs * mixed + ss * grams[b, cols:, cols:]
        gram.append(own * (1.0 / (size * size)) + empty)
    gram = invert(gram)
    for b in range(sectors):
        correlation = ff * corr_ff[b] + fs * corr_x[b] + ss * corr_ss[b]
        own = exact_dot(gram[b], correlation) * (1.0 / size)
        right[b] = own
        right_low[b] = own.astype(bf16)
        image[b] = of_first * images[b, :cols] + of_resid * images[b, cols:]


def plane_groups():
    return [[x * 4 + z * 2 + c for x in range(4) for c in range(2)] for z in range(2)]


def across_seg(array, by):
    segs, ops = lax.axis_size("seg"), lax.axis_size("op")
    pairs = []
    for seg in range(segs):
        for op in range(ops):
            other = op if 0 <= seg + by < segs else op ^ 2
            pairs.append((seg * ops + op, (seg + by) % segs * ops + other))
    return lax.ppermute(array, ("seg", "op"), pairs)


def sum_over_op(part):
    chunks = part.reshape(8, 128, 256)
    chunks = lax.all_to_all(chunks, "op", 0, 0, axis_index_groups=plane_groups(), tiled=True)
    own = jnp.sum(chunks.astype(f32), axis=0).astype(bf16)
    other = lax.ppermute(own, "op", [(i, i ^ 2) for i in range(16)])
    both = (own.astype(f32) + other.astype(f32)).astype(bf16)
    spread = jnp.broadcast_to(both[None], (8, 128, 256))
    whole = lax.all_to_all(spread, "op", 0, 0, axis_index_groups=plane_groups(), tiled=True)
    return whole.reshape(4, 256, 256)


def shards(
    left_part, right_part, inverse_values, left_env, right_env, source, term_active, sketch, kept
):
    lenv, renv = left_env[0], right_env[0]
    slots, sectors = lenv.shape[:2]
    whole, cols = (sectors, 256, 256), sketch.shape[2]
    neighbour = across_seg(right_part[0], -1)
    tests = sketch[0].T
    scaled, lenv_near, renv_near = call(
        prepare_kernel,
        (left_part[0], inverse_values[0], lenv, renv),
        [VMEM, VMEM, HBM, HBM],
        [(whole, bf16), (lenv.shape, bf16), ((sectors, slots * 256, 256), bf16)],
        [VMEM] * 3,
        [pltpu.SemaphoreType.DMA((slots, 2))],
        moved=8_000_000,
    )
    inner = pltpu.VMEM((sectors, 256, slots * 256), bf16)
    first, part, ray = call(
        first_kernel,
        (source, term_active, scaled, neighbour, lenv_near, renv_near),
        [SMEM, SMEM] + [VMEM] * 4,
        [(whole, f32), (whole, bf16), ((8, 128), f32)],
        [HBM, VMEM, VMEM],
        [
            pltpu.VMEM(whole, f32), inner, pltpu.VMEM(whole, bf16), pltpu.VMEM(whole, f32),
            pltpu.SemaphoreType.DMA((sectors,)),
        ],
        flops=940_000_000, moved=6_000_000,
    )
    resid = sum_over_op(part)
    rays, coupling = call(
        second_kernel,
        (source, term_active, resid, ray, lenv, renv),
        [SMEM, SMEM] + [VMEM] * 4,
        [((16, 128), f32), ((8, 128), f32)],
        [VMEM] * 2,
        [inner, pltpu.VMEM(whole, bf16)],
        flops=800_000_000, moved=4_000_000,
    )
    rays = lax.all_to_all(rays, "op", 0, 0, tiled=True)
    quadratic = call(
        quadratic_kernel,
        (kept, first, resid, tests),
        [SMEM] + [VMEM] * 3,
        [((sectors, 2 * cols, 256), f32)] * 2 + [((sectors, cols, 256), f32)] * 3,
        [VMEM] * 5,
        flops=1_600_000_000, moved=6_000_000,
    )
    right, right_low, image = call(
        solve_kernel,
        (kept, rays, coupling) + tuple(quadratic),
        [SMEM] + [VMEM] * 7,
        [((sectors, cols, 256), f32), ((sectors, cols, 256), bf16), ((sectors, cols, 256), f32)],
        [VMEM] * 3,
        flops=800_000_000, moved=5_000_000,
    )
    handed = across_seg(right_low, 1)
    kept_state = jnp.einsum("bki,bkj->bij", image, right, precision=HIGHEST) / 256
    return (kept_state.astype(bf16)[None], handed[None])


def solution(mesh):
    placed = (
        P("seg", None, None, None),
        P("seg", None, None, None),
        P("seg", None, None),
        P("seg", "op", None, None, None),
        P("seg", "op", None, None, None),
        P("op", None),
        P("op"),
        P("seg", None, None),
        P("seg", None),
    )
    return jax.shard_map(
        shards,
        mesh=mesh,
        in_specs=placed,
        out_specs=(P("seg", None, None, None), P("seg", None, None, None)),
        check_vma=False,
    )
```

```python
import jax
import jax.numpy as jnp
from jax import lax
from jax.experimental import pallas as pl
from jax.experimental.pallas import tpu as pltpu
from jax.sharding import PartitionSpec as P

bf16, f32 = jnp.bfloat16, jnp.float32
HIGHEST = lax.Precision.HIGHEST
NN = (((1,), (0,)), ((), ()))
NT = (((1,), (1,)), ((), ()))
AHEAD = 2

SMEM = pl.BlockSpec(memory_space=pltpu.SMEM)
VMEM = pl.BlockSpec(memory_space=pltpu.VMEM)
HBM = pl.BlockSpec(memory_space=pltpu.HBM)


def call(kernel, operands, in_specs, outs, out_specs, scratch=(), flops=0, moved=0):
    return pl.pallas_call(
        kernel,
        out_shape=tuple(jax.ShapeDtypeStruct(shape, dtype) for shape, dtype in outs),
        in_specs=in_specs,
        out_specs=tuple(out_specs),
        scratch_shapes=list(scratch),
        compiler_params=pltpu.CompilerParams(vmem_limit_bytes=24 * 2**20),
        cost_estimate=pl.CostEstimate(flops=flops, bytes_accessed=moved, transcendentals=0),
    )(*operands)


def prepare_kernel(left_part, inverse, sketch, lenv_hbm, renv_hbm, scaled, tests, lenv, renv, sems):
    copies = []
    for slot in range(lenv.shape[0]):
        rows = pl.ds(slot * 256, 256)
        copies.append(pltpu.make_async_copy(lenv_hbm.at[slot], lenv.at[slot], sems.at[slot, 0]))
        copies.append(
            pltpu.make_async_copy(renv_hbm.at[slot], renv.at[:, rows, :], sems.at[slot, 1])
        )
    for copy in copies:
        copy.start()
    for b in range(left_part.shape[0]):
        scaled[b] = (left_part[b].astype(f32) * inverse[b : b + 1, :]).astype(bf16)
    tests[...] = sketch[...].T
    for copy in copies:
        copy.wait()


def first_kernel(
    source, active, scaled, neighbour, lenv, renv,
    first_hbm, part, ray, first, inner, vector, image, sems,
):
    slots, sectors = lenv.shape[:2]
    count = sectors * 256 * 256
    squares = jnp.zeros((1, 256), f32)
    for b in range(sectors):
        center = jnp.dot(scaled[b], neighbour[b], preferred_element_type=f32)
        image[b] = center
        squares += jnp.sum(center * center, axis=0, keepdims=True)
    scale = lax.rsqrt(jnp.sum(squares, axis=1, keepdims=True) / count + 1e-06)
    out_copies = []
    for b in range(sectors):
        scaled_center = image[b] * scale
        first[b] = scaled_center
        out_copies.append(pltpu.make_async_copy(first.at[b], first_hbm.at[b], sems.at[b]))
        out_copies[b].start()
        vector[b] = scaled_center.astype(bf16)
    for slot in range(slots):
        flag = active[slot].astype(f32)
        for b in range(sectors):
            product = jnp.dot(
                lenv[slot, b], vector[source[slot, b]], preferred_element_type=f32
            )
            inner[b, :, slot * 256 : (slot + 1) * 256] = (product * flag).astype(bf16)
    dots = jnp.zeros((1, 256), f32)
    for b in range(sectors):
        own = jnp.dot(inner[b], renv[b], preferred_element_type=f32)
        image[b] = own
        dots += jnp.sum(first[b] * own, axis=0, keepdims=True)
    own_ray = jnp.sum(dots, axis=1, keepdims=True) / count
    for b in range(sectors):
        part[b] = (image[b] - own_ray * first[b]).astype(bf16)
    ray[...] = jnp.broadcast_to(own_ray, ray.shape)
    for copy in out_copies:
        copy.wait()


def sum_kernel(chunks, total):
    summed = chunks[0].astype(f32)
    for i in range(1, chunks.shape[0]):
        summed += chunks[i].astype(f32)
    total[...] = summed.astype(bf16)


def second_kernel(source, active, resid, first_ray, lenv, renv, rays, coupling, inner):
    slots, sectors = lenv.shape[:2]
    count = sectors * 256 * 256
    for slot in range(slots):
        flag = active[slot].astype(f32)
        for b in range(sectors):
            product = jnp.dot(
                lenv[slot, b], resid[source[slot, b]], preferred_element_type=f32
            )
            inner[b, :, slot * 256 : (slot + 1) * 256] = (product * flag).astype(bf16)
    dots, squares = jnp.zeros((1, 256), f32), jnp.zeros((1, 256), f32)
    for b in range(sectors):
        below = jnp.concatenate([renv[slot, b] for slot in range(slots)], axis=0)
        own = jnp.dot(inner[b], below, preferred_element_type=f32)
        piece = resid[b].astype(f32)
        dots += jnp.sum(piece * own, axis=0, keepdims=True)
        squares += jnp.sum(piece * piece, axis=0, keepdims=True)
    mean_square = jnp.sum(squares, axis=1, keepdims=True) / count + 1e-06
    own_ray = jnp.sum(dots, axis=1, keepdims=True) / count / mean_square
    lane = lax.broadcasted_iota(jnp.int32, rays.shape, 1)
    rays[...] = jnp.where(lane == 0, first_ray[0:1, :], jnp.broadcast_to(own_ray, rays.shape))
    coupling[...] = jnp.broadcast_to(jnp.sqrt(mean_square), coupling.shape)


def split(array):
    high = array.astype(bf16)
    return high, (array - high.astype(f32)).astype(bf16)


def dot(left, right, dims=NN):
    return lax.dot_general(left, right, dims, preferred_element_type=f32)


def fine_dot(left, right, dims=NN):
    return dot(left[0], right[0], dims) + (
        dot(left[0], right[1], dims) + dot(left[1], right[0], dims)
    )


def exact_dot(left, right, dims=NN):
    return lax.dot_general(left, right, dims, precision=HIGHEST, preferred_element_type=f32)


def quadratic_kernel(
    kept, first, resid, sketch, images, gram_ff, gram_x, gram_ss, corr_ff, corr_x, corr_ss
):
    sectors, size = first.shape[:2]
    cols = sketch.shape[0]
    tests = split(sketch[...])
    row = lax.broadcasted_iota(jnp.int32, (cols, size), 0)
    for b in range(sectors):
        wide = row < kept[0, b]
        other = resid[b]
        ground = split(first[b])
        of_first = jnp.where(wide, fine_dot(tests, ground, NT), 0.0)
        of_resid = jnp.where(wide, dot(tests[0], other, NT) + dot(tests[1], other, NT), 0.0)
        images[b, :cols] = of_first
        images[b, cols:] = of_resid
        both = split(images[b])
        gram = fine_dot(both, both, NT)
        gram_ff[b] = gram[:cols, :cols]
        gram_x[b] = gram[:cols, cols:] + gram[cols:, :cols]
        gram_ss[b] = gram[cols:, cols:]
        with_first = fine_dot(both, ground)
        with_resid = dot(both[0], other) + dot(both[1], other)
        corr_ff[b] = with_first[:cols]
        corr_x[b] = with_first[cols:] + with_resid[:cols]
        corr_ss[b] = with_resid[cols:]


def invert_blocks(packed):
    size = packed.shape[0]
    row = lax.broadcasted_iota(jnp.int32, packed.shape, 0)
    lane = lax.broadcasted_iota(jnp.int32, packed.shape, 1)
    place = lane % size
    start = lane - place
    spot = place[0:1, :]

    def column(array, k):
        return jnp.take_along_axis(array, start + k, axis=1)

    queue = [(column(packed, k), column(packed, k + 1)) for k in range(0, 2 * AHEAD, 2)]
    for k in range(0, size, 2):
        left, right = queue.pop(0)
        if k + 2 * AHEAD < size:
            queue.append((column(packed, k + 2 * AHEAD), column(packed, k + 2 * AHEAD + 1)))
        top, cross, low = left[k : k + 1, :], left[k + 1 : k + 2, :], right[k + 1 : k + 2, :]
        scale = 1.0 / (top * low - cross * cross)
        top, cross, low = top * scale, cross * scale, low * scale
        upper = jnp.where(spot == k, 1.0, jnp.where(spot == k + 1, 0.0, packed[k : k + 1, :]))
        lower = jnp.where(spot == k, 0.0, jnp.where(spot == k + 1, 1.0, packed[k + 1 : k + 2, :]))
        upper, lower = low * upper - cross * lower, top * lower - cross * upper
        packed = jnp.where((place == k) | (place == k + 1), 0.0, packed)
        packed = packed - left * upper - right * lower
        packed = jnp.where(row == k, upper, jnp.where(row == k + 1, lower, packed))
        for place_in_queue, pair in enumerate(queue):
            news = []
            for side, old in enumerate(pair):
                j = k + 2 * place_in_queue + 2 + side
                first, second = left[j : j + 1, :], right[j : j + 1, :]
                first, second = low * first - cross * second, top * second - cross * first
                new = old - left * first - right * second
                news.append(jnp.where(row == k, first, jnp.where(row == k + 1, second, new)))
            queue[place_in_queue] = tuple(news)
    return packed


def invert(gram):
    sectors, cols, size = len(gram), gram[0].shape[0], 32
    row = lax.broadcasted_iota(jnp.int32, (cols, cols), 0)
    lane = lax.broadcasted_iota(jnp.int32, (cols, cols), 1)
    same = (row // size) == (lane // size)
    unit = jnp.where(row % size == lane % size, 1.0, 0.0).astype(f32)
    block_lane = lax.broadcasted_iota(jnp.int32, (size, cols), 1) // size
    for p in range(cols // size):
        rows = slice(p * size, (p + 1) * size)
        packed = jnp.zeros((size, cols), f32)
        for s in range(sectors):
            shift = ((s - p) * size) % cols
            turned = pltpu.roll(gram[s][rows], shift, 1) if shift else gram[s][rows]
            packed = jnp.where(block_lane == s, turned, packed)
        inverse = invert_blocks(packed)
        inverse = jnp.where(same, jnp.concatenate([inverse] * sectors, axis=0), 0.0)
        stacked = jnp.concatenate([g[rows] for g in gram], axis=0)
        stacked = jnp.where(lane // size == p, unit, stacked)
        panel = exact_dot(inverse, stacked)
        for s in range(sectors):
            own = panel[s * size : (s + 1) * size]
            tiled = jnp.concatenate([own] * (cols // size), axis=0)
            factor = jnp.where((lane // size == p) & (row // size != p), gram[s], 0.0)
            rest = jnp.where(lane // size == p, 0.0, gram[s])
            rest = jnp.where(row // size == p, tiled, rest)
            gram[s] = rest - exact_dot(factor, tiled)
    return gram


def solve_kernel(
    kept, rays, coupling, images, gram_ff, gram_x, gram_ss, corr_ff, corr_x, corr_ss,
    right, right_low, image,
):
    sectors, size = corr_x.shape[0], corr_x.shape[2]
    cols = corr_x.shape[1]
    sums = jnp.sum(rays[...], axis=0, keepdims=True)
    ray_first, ray_second = sums[:, 0:1], sums[:, 1:2]
    between = coupling[0:1, 0:1]
    half = 0.5 * (ray_second - ray_first)
    weight = half + jnp.sqrt(half * half + between * between)
    length = lax.rsqrt(weight * weight + between * between)
    of_first, of_resid = weight * length, -length
    ff, fs, ss = of_first * of_first, of_first * of_resid, of_resid * of_resid
    row = lax.broadcasted_iota(jnp.int32, (cols, cols), 0)
    lane = lax.broadcasted_iota(jnp.int32, (cols, cols), 1)
    gram = []
    for b in range(sectors):
        empty = jnp.where((row == lane) & (row >= kept[0, b]), 1.0, 0.0)
        own = ff * gram_ff[b] + fs * gram_x[b] + ss * gram_ss[b]
        gram.append(own * (1.0 / (size * size)) + empty)
    gram = invert(gram)
    for b in range(sectors):
        correlation = ff * corr_ff[b] + fs * corr_x[b] + ss * corr_ss[b]
        own = exact_dot(gram[b], correlation) * (1.0 / size)
        right[b] = own
        right_low[b] = own.astype(bf16)
        image[b] = of_first * images[b, :cols] + of_resid * images[b, cols:]


def plane_groups():
    return [[x * 4 + z * 2 + c for x in range(4) for c in range(2)] for z in range(2)]


def across_seg(array, by, swap):
    segs, ops = lax.axis_size("seg"), lax.axis_size("op")
    pairs = []
    for seg in range(segs):
        for op in range(ops):
            other = op ^ 2 if swap and not 0 <= seg + by < segs else op
            pairs.append((seg * ops + op, (seg + by) % segs * ops + other))
    return lax.ppermute(array, ("seg", "op"), pairs)


def sum_over_op(part):
    chunks = part.reshape(8, 128, 256)
    chunks = lax.all_to_all(chunks, "op", 0, 0, axis_index_groups=plane_groups(), tiled=True)
    (own,) = call(
        sum_kernel, (chunks,), [VMEM], [((128, 256), bf16)], [VMEM], flops=1_000_000, moved=600_000
    )
    other = lax.ppermute(own, "op", [(i, i ^ 2) for i in range(16)])
    both = (own.astype(f32) + other.astype(f32)).astype(bf16)
    spread = jnp.broadcast_to(both[None], (8, 128, 256))
    whole = lax.all_to_all(spread, "op", 0, 0, axis_index_groups=plane_groups(), tiled=True)
    return whole.reshape(4, 256, 256)


def shards(
    left_part, right_part, inverse_values, left_env, right_env, source, term_active, sketch, kept
):
    lenv, renv = left_env[0], right_env[0]
    slots, sectors = lenv.shape[:2]
    whole, cols = (sectors, 256, 256), sketch.shape[2]
    neighbour = across_seg(right_part, -1, False)[0]
    scaled, tests, lenv_near, renv_near = call(
        prepare_kernel,
        (left_part[0], inverse_values[0], sketch[0], lenv, renv),
        [VMEM] * 3 + [HBM] * 2,
        [(whole, bf16), ((cols, 256), f32), (lenv.shape, bf16), ((sectors, slots * 256, 256), bf16)],
        [VMEM] * 4,
        [pltpu.SemaphoreType.DMA((slots, 2))],
        moved=8_000_000,
    )
    inner = pltpu.VMEM((sectors, 256, slots * 256), bf16)
    first, part, ray = call(
        first_kernel,
        (source, term_active, scaled, neighbour, lenv_near, renv_near),
        [SMEM, SMEM] + [VMEM] * 4,
        [(whole, f32), (whole, bf16), ((8, 128), f32)],
        [HBM, VMEM, VMEM],
        [
            pltpu.VMEM(whole, f32), inner, pltpu.VMEM(whole, bf16), pltpu.VMEM(whole, f32),
            pltpu.SemaphoreType.DMA((sectors,)),
        ],
        flops=940_000_000, moved=6_000_000,
    )
    resid = sum_over_op(part)
    rays, coupling = call(
        second_kernel,
        (source, term_active, resid, ray, lenv, renv),
        [SMEM, SMEM] + [VMEM] * 4,
        [((16, 128), f32), ((8, 128), f32)],
        [VMEM] * 2,
        [inner],
        flops=800_000_000, moved=4_000_000,
    )
    rays = lax.all_to_all(rays, "op", 0, 0, tiled=True)
    quadratic = call(
        quadratic_kernel,
        (kept, first, resid, tests),
        [SMEM] + [VMEM] * 3,
        [((sectors, 2 * cols, 256), f32)]
        + [((sectors, cols, cols), f32)] * 3
        + [((sectors, cols, 256), f32)] * 3,
        [VMEM] * 7,
        flops=1_600_000_000, moved=6_000_000,
    )
    right, right_low, image = call(
        solve_kernel,
        (kept, rays, coupling) + tuple(quadratic),
        [SMEM] + [VMEM] * 9,
        [((sectors, cols, 256), f32), ((sectors, cols, 256), bf16), ((sectors, cols, 256), f32)],
        [VMEM] * 3,
        flops=800_000_000, moved=5_000_000,
    )
    handed = across_seg(right_low[None], 1, True)
    kept_state = jnp.einsum("bki,bkj->bij", image, right, precision=HIGHEST) / 256
    return (kept_state.astype(bf16)[None], handed)


def solution(mesh):
    placed = (
        P("seg", None, None, None),
        P("seg", None, None, None),
        P("seg", None, None),
        P("seg", "op", None, None, None),
        P("seg", "op", None, None, None),
        P("op", None),
        P("op"),
        P("seg", None, None),
        P("seg", None),
    )
    return jax.shard_map(
        shards,
        mesh=mesh,
        in_specs=placed,
        out_specs=(P("seg", None, None, None), P("seg", None, None, None)),
        check_vma=False,
    )
```

```python
import jax
import jax.numpy as jnp
from jax import lax
from jax.experimental import pallas as pl
from jax.experimental.pallas import tpu as pltpu
from jax.sharding import PartitionSpec as P

bf16, f32 = jnp.bfloat16, jnp.float32
HIGHEST = lax.Precision.HIGHEST
NN = (((1,), (0,)), ((), ()))
NT = (((1,), (1,)), ((), ()))
AHEAD = 2

SMEM = pl.BlockSpec(memory_space=pltpu.SMEM)
VMEM = pl.BlockSpec(memory_space=pltpu.VMEM)
HBM = pl.BlockSpec(memory_space=pltpu.HBM)


def call(kernel, operands, in_specs, outs, out_specs, scratch=(), flops=0, moved=0):
    return pl.pallas_call(
        kernel,
        out_shape=tuple(jax.ShapeDtypeStruct(shape, dtype) for shape, dtype in outs),
        in_specs=in_specs,
        out_specs=tuple(out_specs),
        scratch_shapes=list(scratch),
        compiler_params=pltpu.CompilerParams(vmem_limit_bytes=24 * 2**20),
        cost_estimate=pl.CostEstimate(flops=flops, bytes_accessed=moved, transcendentals=0),
    )(*operands)


def prepare_kernel(left_part, inverse, sketch, lenv_hbm, renv_hbm, scaled, tests, lenv, renv, sems):
    copies = []
    for slot in range(lenv.shape[0]):
        rows = pl.ds(slot * 256, 256)
        copies.append(pltpu.make_async_copy(lenv_hbm.at[slot], lenv.at[slot], sems.at[slot, 0]))
        copies.append(
            pltpu.make_async_copy(renv_hbm.at[slot], renv.at[:, rows, :], sems.at[slot, 1])
        )
    for copy in copies:
        copy.start()
    for b in range(left_part.shape[0]):
        scaled[b] = (left_part[b].astype(f32) * inverse[b : b + 1, :]).astype(bf16)
    tests[...] = sketch[...].T
    for copy in copies:
        copy.wait()


def first_kernel(
    source, active, scaled, neighbour, lenv, renv,
    first_hbm, part, ray, first, inner, vector, image, sems,
):
    slots, sectors = lenv.shape[:2]
    count = sectors * 256 * 256
    squares = jnp.zeros((1, 256), f32)
    for b in range(sectors):
        center = jnp.dot(scaled[b], neighbour[b], preferred_element_type=f32)
        image[b] = center
        squares += jnp.sum(center * center, axis=0, keepdims=True)
    scale = lax.rsqrt(jnp.sum(squares, axis=1, keepdims=True) / count + 1e-06)
    out_copies = []
    for b in range(sectors):
        scaled_center = image[b] * scale
        first[b] = scaled_center
        out_copies.append(pltpu.make_async_copy(first.at[b], first_hbm.at[b], sems.at[b]))
        out_copies[b].start()
        vector[b] = scaled_center.astype(bf16)
    for slot in range(slots):
        flag = active[slot].astype(f32)
        for b in range(sectors):
            product = jnp.dot(
                lenv[slot, b], vector[source[slot, b]], preferred_element_type=f32
            )
            inner[b, :, slot * 256 : (slot + 1) * 256] = (product * flag).astype(bf16)
    dots = jnp.zeros((1, 256), f32)
    for b in range(sectors):
        own = jnp.dot(inner[b], renv[b], preferred_element_type=f32)
        image[b] = own
        dots += jnp.sum(first[b] * own, axis=0, keepdims=True)
    own_ray = jnp.sum(dots, axis=1, keepdims=True) / count
    for b in range(sectors):
        part[b] = (image[b] - own_ray * first[b]).astype(bf16)
    ray[...] = jnp.broadcast_to(own_ray, ray.shape)
    for copy in out_copies:
        copy.wait()


def sum_kernel(chunks, total):
    summed = chunks[0].astype(f32)
    for i in range(1, chunks.shape[0]):
        summed += chunks[i].astype(f32)
    total[...] = summed.astype(bf16)


def second_kernel(source, active, resid, first_ray, lenv, renv, rays, coupling, inner):
    slots, sectors = lenv.shape[:2]
    count = sectors * 256 * 256
    for slot in range(slots):
        flag = active[slot].astype(f32)
        for b in range(sectors):
            product = jnp.dot(
                lenv[slot, b], resid[source[slot, b]], preferred_element_type=f32
            )
            inner[b, :, slot * 256 : (slot + 1) * 256] = (product * flag).astype(bf16)
    dots, squares = jnp.zeros((1, 256), f32), jnp.zeros((1, 256), f32)
    for b in range(sectors):
        below = jnp.concatenate([renv[slot, b] for slot in range(slots)], axis=0)
        own = jnp.dot(inner[b], below, preferred_element_type=f32)
        piece = resid[b].astype(f32)
        dots += jnp.sum(piece * own, axis=0, keepdims=True)
        squares += jnp.sum(piece * piece, axis=0, keepdims=True)
    mean_square = jnp.sum(squares, axis=1, keepdims=True) / count + 1e-06
    own_ray = jnp.sum(dots, axis=1, keepdims=True) / count / mean_square
    lane = lax.broadcasted_iota(jnp.int32, rays.shape, 1)
    rays[...] = jnp.where(lane == 0, first_ray[0:1, :], jnp.broadcast_to(own_ray, rays.shape))
    coupling[...] = jnp.broadcast_to(jnp.sqrt(mean_square), coupling.shape)


def split(array):
    high = array.astype(bf16)
    return high, (array - high.astype(f32)).astype(bf16)


def dot(left, right, dims=NN):
    return lax.dot_general(left, right, dims, preferred_element_type=f32)


def fine_dot(left, right, dims=NN):
    return dot(left[0], right[0], dims) + (
        dot(left[0], right[1], dims) + dot(left[1], right[0], dims)
    )


def exact_dot(left, right, dims=NN):
    return lax.dot_general(left, right, dims, precision=HIGHEST, preferred_element_type=f32)


def invert_blocks(packed):
    size = packed.shape[0]
    row = lax.broadcasted_iota(jnp.int32, packed.shape, 0)
    lane = lax.broadcasted_iota(jnp.int32, packed.shape, 1)
    place = lane % size
    start = lane - place
    spot = place[0:1, :]

    def column(array, k):
        return jnp.take_along_axis(array, start + k, axis=1)

    queue = [(column(packed, k), column(packed, k + 1)) for k in range(0, 2 * AHEAD, 2)]
    for k in range(0, size, 2):
        left, right = queue.pop(0)
        if k + 2 * AHEAD < size:
            queue.append((column(packed, k + 2 * AHEAD), column(packed, k + 2 * AHEAD + 1)))
        top, cross, low = left[k : k + 1, :], left[k + 1 : k + 2, :], right[k + 1 : k + 2, :]
        scale = 1.0 / (top * low - cross * cross)
        top, cross, low = top * scale, cross * scale, low * scale
        upper = jnp.where(spot == k, 1.0, jnp.where(spot == k + 1, 0.0, packed[k : k + 1, :]))
        lower = jnp.where(spot == k, 0.0, jnp.where(spot == k + 1, 1.0, packed[k + 1 : k + 2, :]))
        upper, lower = low * upper - cross * lower, top * lower - cross * upper
        packed = jnp.where((place == k) | (place == k + 1), 0.0, packed)
        packed = packed - left * upper - right * lower
        packed = jnp.where(row == k, upper, jnp.where(row == k + 1, lower, packed))
        for place_in_queue, pair in enumerate(queue):
            news = []
            for side, old in enumerate(pair):
                j = k + 2 * place_in_queue + 2 + side
                first, second = left[j : j + 1, :], right[j : j + 1, :]
                first, second = low * first - cross * second, top * second - cross * first
                new = old - left * first - right * second
                news.append(jnp.where(row == k, first, jnp.where(row == k + 1, second, new)))
            queue[place_in_queue] = tuple(news)
    return packed


def invert(gram):
    sectors, cols, size = len(gram), gram[0].shape[0], 32
    row = lax.broadcasted_iota(jnp.int32, (cols, cols), 0)
    lane = lax.broadcasted_iota(jnp.int32, (cols, cols), 1)
    same = (row // size) == (lane // size)
    unit = jnp.where(row % size == lane % size, 1.0, 0.0).astype(f32)
    block_lane = lax.broadcasted_iota(jnp.int32, (size, cols), 1) // size
    for p in range(cols // size):
        rows = slice(p * size, (p + 1) * size)
        packed = jnp.zeros((size, cols), f32)
        for s in range(sectors):
            shift = ((s - p) * size) % cols
            turned = pltpu.roll(gram[s][rows], shift, 1) if shift else gram[s][rows]
            packed = jnp.where(block_lane == s, turned, packed)
        inverse = invert_blocks(packed)
        inverse = jnp.where(same, jnp.concatenate([inverse] * sectors, axis=0), 0.0)
        stacked = jnp.concatenate([g[rows] for g in gram], axis=0)
        stacked = jnp.where(lane // size == p, unit, stacked)
        panel = exact_dot(inverse, stacked)
        for s in range(sectors):
            own = panel[s * size : (s + 1) * size]
            tiled = jnp.concatenate([own] * (cols // size), axis=0)
            factor = jnp.where((lane // size == p) & (row // size != p), gram[s], 0.0)
            rest = jnp.where(lane // size == p, 0.0, gram[s])
            rest = jnp.where(row // size == p, tiled, rest)
            gram[s] = rest - exact_dot(factor, tiled)
    return gram


def truncate_kernel(kept, rays, coupling, first, resid, sketch, right, right_low, image):
    sectors, size = first.shape[:2]
    cols = sketch.shape[0]
    sums = jnp.sum(rays[...], axis=0, keepdims=True)
    ray_first, ray_second = sums[:, 0:1], sums[:, 1:2]
    between = coupling[0:1, 0:1]
    half = 0.5 * (ray_second - ray_first)
    weight = half + jnp.sqrt(half * half + between * between)
    length = lax.rsqrt(weight * weight + between * between)
    of_first, of_resid = weight * length, length
    tests = split(sketch[...])
    row = lax.broadcasted_iota(jnp.int32, (cols, cols), 0)
    lane = lax.broadcasted_iota(jnp.int32, (cols, cols), 1)
    wide_row = lax.broadcasted_iota(jnp.int32, (cols, size), 0)
    gram, correlation = [], []
    for b in range(sectors):
        ground = split(of_first * first[b] - of_resid * resid[b].astype(f32))
        own = jnp.where(wide_row < kept[0, b], fine_dot(tests, ground, NT), 0.0)
        image[b] = own
        own = split(own)
        empty = jnp.where((row == lane) & (row >= kept[0, b]), 1.0, 0.0)
        gram.append(fine_dot(own, own, NT) * (1.0 / (size * size)) + empty)
        correlation.append(fine_dot(own, ground))
    gram = invert(gram)
    for b in range(sectors):
        own = exact_dot(gram[b], correlation[b]) * (1.0 / size)
        right[b] = own
        right_low[b] = own.astype(bf16)


def plane_groups():
    return [[x * 4 + z * 2 + c for x in range(4) for c in range(2)] for z in range(2)]


def across_seg(array, by, swap):
    segs, ops = lax.axis_size("seg"), lax.axis_size("op")
    pairs = []
    for seg in range(segs):
        for op in range(ops):
            other = op ^ 2 if swap and not 0 <= seg + by < segs else op
            pairs.append((seg * ops + op, (seg + by) % segs * ops + other))
    return lax.ppermute(array, ("seg", "op"), pairs)


def sum_over_op(part):
    chunks = part.reshape(8, 128, 256)
    chunks = lax.all_to_all(chunks, "op", 0, 0, axis_index_groups=plane_groups(), tiled=True)
    (own,) = call(
        sum_kernel, (chunks,), [VMEM], [((128, 256), bf16)], [VMEM], flops=1_000_000, moved=600_000
    )
    other = lax.ppermute(own, "op", [(i, i ^ 2) for i in range(16)])
    both = (own.astype(f32) + other.astype(f32)).astype(bf16)
    spread = jnp.broadcast_to(both[None], (8, 128, 256))
    whole = lax.all_to_all(spread, "op", 0, 0, axis_index_groups=plane_groups(), tiled=True)
    return whole.reshape(4, 256, 256)


def shards(
    left_part, right_part, inverse_values, left_env, right_env, source, term_active, sketch, kept
):
    lenv, renv = left_env[0], right_env[0]
    slots, sectors = lenv.shape[:2]
    whole, cols = (sectors, 256, 256), sketch.shape[2]
    neighbour = across_seg(right_part, -1, False)[0]
    scaled, tests, lenv_near, renv_near = call(
        prepare_kernel,
        (left_part[0], inverse_values[0], sketch[0], lenv, renv),
        [VMEM] * 3 + [HBM] * 2,
        [(whole, bf16), ((cols, 256), f32), (lenv.shape, bf16), ((sectors, slots * 256, 256), bf16)],
        [VMEM] * 4,
        [pltpu.SemaphoreType.DMA((slots, 2))],
        moved=8_000_000,
    )
    inner = pltpu.VMEM((sectors, 256, slots * 256), bf16)
    first, part, ray = call(
        first_kernel,
        (source, term_active, scaled, neighbour, lenv_near, renv_near),
        [SMEM, SMEM] + [VMEM] * 4,
        [(whole, f32), (whole, bf16), ((8, 128), f32)],
        [HBM, VMEM, VMEM],
        [
            pltpu.VMEM(whole, f32), inner, pltpu.VMEM(whole, bf16), pltpu.VMEM(whole, f32),
            pltpu.SemaphoreType.DMA((sectors,)),
        ],
        flops=940_000_000, moved=6_000_000,
    )
    resid = sum_over_op(part)
    rays, coupling = call(
        second_kernel,
        (source, term_active, resid, ray, lenv, renv),
        [SMEM, SMEM] + [VMEM] * 4,
        [((16, 128), f32), ((8, 128), f32)],
        [VMEM] * 2,
        [inner],
        flops=800_000_000, moved=4_000_000,
    )
    rays = lax.all_to_all(rays, "op", 0, 0, tiled=True)
    right, right_low, image = call(
        truncate_kernel,
        (kept, rays, coupling, first, resid, tests),
        [SMEM] + [VMEM] * 5,
        [((sectors, cols, 256), f32), ((sectors, cols, 256), bf16), ((sectors, cols, 256), f32)],
        [VMEM] * 3,
        flops=1_200_000_000, moved=4_000_000,
    )
    handed = across_seg(right_low[None], 1, True)
    kept_state = jnp.einsum("bki,bkj->bij", image, right, precision=HIGHEST) / 256
    return (kept_state.astype(bf16)[None], handed)


def solution(mesh):
    placed = (
        P("seg", None, None, None),
        P("seg", None, None, None),
        P("seg", None, None),
        P("seg", "op", None, None, None),
        P("seg", "op", None, None, None),
        P("op", None),
        P("op"),
        P("seg", None, None),
        P("seg", None),
    )
    return jax.shard_map(
        shards,
        mesh=mesh,
        in_specs=placed,
        out_specs=(P("seg", None, None, None), P("seg", None, None, None)),
        check_vma=False,
    )
```

```python
import jax
import jax.numpy as jnp
from jax import lax
from jax.experimental import pallas as pl
from jax.experimental.pallas import tpu as pltpu
from jax.sharding import PartitionSpec as P

bf16, f32 = jnp.bfloat16, jnp.float32
HIGHEST = lax.Precision.HIGHEST
NN = (((1,), (0,)), ((), ()))
NT = (((1,), (1,)), ((), ()))
AHEAD = 2

SMEM = pl.BlockSpec(memory_space=pltpu.SMEM)
VMEM = pl.BlockSpec(memory_space=pltpu.VMEM)
HBM = pl.BlockSpec(memory_space=pltpu.HBM)


def call(kernel, operands, in_specs, outs, out_specs, scratch=(), flops=0, moved=0):
    return pl.pallas_call(
        kernel,
        out_shape=tuple(jax.ShapeDtypeStruct(shape, dtype) for shape, dtype in outs),
        in_specs=in_specs,
        out_specs=tuple(out_specs),
        scratch_shapes=list(scratch),
        compiler_params=pltpu.CompilerParams(vmem_limit_bytes=24 * 2**20),
        cost_estimate=pl.CostEstimate(flops=flops, bytes_accessed=moved, transcendentals=0),
    )(*operands)


def prepare_kernel(left_part, inverse, sketch, lenv_hbm, renv_hbm, scaled, tests, lenv, renv, sems):
    copies = []
    for slot in range(lenv.shape[0]):
        rows = pl.ds(slot * 256, 256)
        copies.append(pltpu.make_async_copy(lenv_hbm.at[slot], lenv.at[slot], sems.at[slot, 0]))
        copies.append(
            pltpu.make_async_copy(renv_hbm.at[slot], renv.at[:, rows, :], sems.at[slot, 1])
        )
    for copy in copies:
        copy.start()
    for b in range(left_part.shape[0]):
        scaled[b] = (left_part[b].astype(f32) * inverse[b : b + 1, :]).astype(bf16)
    tests[...] = sketch[...].T
    for copy in copies:
        copy.wait()


def first_kernel(
    source, active, scaled, neighbour, lenv, renv,
    first_hbm, part, ray, first, inner, vector, image, sems,
):
    slots, sectors = lenv.shape[:2]
    count = sectors * 256 * 256
    squares = jnp.zeros((1, 256), f32)
    for b in range(sectors):
        center = jnp.dot(scaled[b], neighbour[b], preferred_element_type=f32)
        image[b] = center
        squares += jnp.sum(center * center, axis=0, keepdims=True)
    scale = lax.rsqrt(jnp.sum(squares, axis=1, keepdims=True) / count + 1e-06)
    out_copies = []
    for b in range(sectors):
        scaled_center = image[b] * scale
        first[b] = scaled_center
        out_copies.append(pltpu.make_async_copy(first.at[b], first_hbm.at[b], sems.at[b]))
        out_copies[b].start()
        vector[b] = scaled_center.astype(bf16)
    for slot in range(slots):
        flag = active[slot].astype(f32)
        for b in range(sectors):
            product = jnp.dot(
                lenv[slot, b], vector[source[slot, b]], preferred_element_type=f32
            )
            inner[b, :, slot * 256 : (slot + 1) * 256] = (product * flag).astype(bf16)
    dots = jnp.zeros((1, 256), f32)
    for b in range(sectors):
        own = jnp.dot(inner[b], renv[b], preferred_element_type=f32)
        image[b] = own
        dots += jnp.sum(first[b] * own, axis=0, keepdims=True)
    own_ray = jnp.sum(dots, axis=1, keepdims=True) / count
    for b in range(sectors):
        part[b] = (image[b] - own_ray * first[b]).astype(bf16)
    ray[...] = jnp.broadcast_to(own_ray, ray.shape)
    for copy in out_copies:
        copy.wait()


def sum_kernel(chunks, total):
    summed = chunks[0].astype(f32)
    for i in range(1, chunks.shape[0]):
        summed += chunks[i].astype(f32)
    total[...] = summed.astype(bf16)


def second_kernel(source, active, resid, first_ray, lenv, renv, rays, coupling, inner):
    slots, sectors = lenv.shape[:2]
    count = sectors * 256 * 256
    for slot in range(slots):
        flag = active[slot].astype(f32)
        for b in range(sectors):
            product = jnp.dot(
                lenv[slot, b], resid[source[slot, b]], preferred_element_type=f32
            )
            inner[b, :, slot * 256 : (slot + 1) * 256] = (product * flag).astype(bf16)
    dots, squares = jnp.zeros((1, 256), f32), jnp.zeros((1, 256), f32)
    for b in range(sectors):
        below = jnp.concatenate([renv[slot, b] for slot in range(slots)], axis=0)
        own = jnp.dot(inner[b], below, preferred_element_type=f32)
        piece = resid[b].astype(f32)
        dots += jnp.sum(piece * own, axis=0, keepdims=True)
        squares += jnp.sum(piece * piece, axis=0, keepdims=True)
    mean_square = jnp.sum(squares, axis=1, keepdims=True) / count + 1e-06
    own_ray = jnp.sum(dots, axis=1, keepdims=True) / count / mean_square
    lane = lax.broadcasted_iota(jnp.int32, rays.shape, 1)
    rays[...] = jnp.where(lane == 0, first_ray[0:1, :], jnp.broadcast_to(own_ray, rays.shape))
    coupling[...] = jnp.broadcast_to(jnp.sqrt(mean_square), coupling.shape)


def split(array):
    high = array.astype(bf16)
    return high, (array - high.astype(f32)).astype(bf16)


def dot(left, right, dims=NN):
    return lax.dot_general(left, right, dims, preferred_element_type=f32)


def fine_dot(left, right, dims=NN):
    return dot(left[0], right[0], dims) + (
        dot(left[0], right[1], dims) + dot(left[1], right[0], dims)
    )


def invert_blocks(packed):
    size = packed.shape[0]
    row = lax.broadcasted_iota(jnp.int32, packed.shape, 0)
    lane = lax.broadcasted_iota(jnp.int32, packed.shape, 1)
    place = lane % size
    start = lane - place
    spot = place[0:1, :]

    def column(array, k):
        return jnp.take_along_axis(array, start + k, axis=1)

    queue = [(column(packed, k), column(packed, k + 1)) for k in range(0, 2 * AHEAD, 2)]
    for k in range(0, size, 2):
        left, right = queue.pop(0)
        if k + 2 * AHEAD < size:
            queue.append((column(packed, k + 2 * AHEAD), column(packed, k + 2 * AHEAD + 1)))
        top, cross, low = left[k : k + 1, :], left[k + 1 : k + 2, :], right[k + 1 : k + 2, :]
        scale = 1.0 / (top * low - cross * cross)

        def eliminate(old, upper, lower):
            upper, lower = low * upper - cross * lower, top * lower - cross * upper
            new = old - (left * upper + right * lower) * scale
            return jnp.where(
                row == k, upper * scale, jnp.where(row == k + 1, lower * scale, new)
            )

        upper = jnp.where(spot == k, 1.0, jnp.where(spot == k + 1, 0.0, packed[k : k + 1, :]))
        lower = jnp.where(spot == k, 0.0, jnp.where(spot == k + 1, 1.0, packed[k + 1 : k + 2, :]))
        rest = jnp.where((place == k) | (place == k + 1), 0.0, packed)
        packed = eliminate(rest, upper, lower)
        for i, pair in enumerate(queue):
            j = k + 2 * i + 2
            queue[i] = tuple(
                eliminate(old, left[n : n + 1, :], right[n : n + 1, :])
                for old, n in zip(pair, (j, j + 1), strict=True)
            )
    return packed


def invert(gram):
    sectors, cols, size = len(gram), gram[0].shape[0], 32
    row = lax.broadcasted_iota(jnp.int32, (cols, cols), 0)
    lane = lax.broadcasted_iota(jnp.int32, (cols, cols), 1)
    same = (row // size) == (lane // size)
    unit = jnp.where(row % size == lane % size, 1.0, 0.0).astype(f32)
    block_lane = lax.broadcasted_iota(jnp.int32, (size, cols), 1) // size
    for p in range(cols // size):
        rows = slice(p * size, (p + 1) * size)
        packed = jnp.zeros((size, cols), f32)
        for s in range(sectors):
            shift = ((s - p) * size) % cols
            turned = pltpu.roll(gram[s][rows], shift, 1) if shift else gram[s][rows]
            packed = jnp.where(block_lane == s, turned, packed)
        inverse = invert_blocks(packed)
        inverse = jnp.where(same, jnp.concatenate([inverse] * sectors, axis=0), 0.0)
        stacked = jnp.concatenate([g[rows] for g in gram], axis=0)
        stacked = jnp.where(lane // size == p, unit, stacked)
        panel = fine_dot(split(inverse), split(stacked))
        for s in range(sectors):
            own = panel[s * size : (s + 1) * size]
            tiled = jnp.concatenate([own] * (cols // size), axis=0)
            factor = jnp.where((lane // size == p) & (row // size != p), gram[s], 0.0)
            rest = jnp.where(lane // size == p, 0.0, gram[s])
            rest = jnp.where(row // size == p, tiled, rest)
            gram[s] = rest - fine_dot(split(factor), split(tiled))
    return gram


def truncate_kernel(kept, rays, coupling, first, resid, sketch, right, right_low, image):
    sectors, size = first.shape[:2]
    cols = sketch.shape[0]
    sums = jnp.sum(rays[...], axis=0, keepdims=True)
    ray_first, ray_second = sums[:, 0:1], sums[:, 1:2]
    between = coupling[0:1, 0:1]
    half = 0.5 * (ray_second - ray_first)
    weight = half + jnp.sqrt(half * half + between * between)
    length = lax.rsqrt(weight * weight + between * between)
    of_first, of_resid = weight * length, length
    tests = split(sketch[...])
    row = lax.broadcasted_iota(jnp.int32, (cols, cols), 0)
    lane = lax.broadcasted_iota(jnp.int32, (cols, cols), 1)
    wide_row = lax.broadcasted_iota(jnp.int32, (cols, size), 0)
    gram, correlation = [], []
    for b in range(sectors):
        ground = split(of_first * first[b] - of_resid * resid[b].astype(f32))
        own = jnp.where(wide_row < kept[0, b], fine_dot(tests, ground, NT), 0.0)
        image[b] = own
        own = split(own)
        empty = jnp.where((row == lane) & (row >= kept[0, b]), 1.0, 0.0)
        gram.append(fine_dot(own, own, NT) * (1.0 / (size * size)) + empty)
        correlation.append(fine_dot(own, ground))
    gram = invert(gram)
    for b in range(sectors):
        own = fine_dot(split(gram[b]), split(correlation[b])) * (1.0 / size)
        right[b] = own
        right_low[b] = own.astype(bf16)


def plane_groups():
    return [[x * 4 + z * 2 + c for x in range(4) for c in range(2)] for z in range(2)]


def upper_half_first():
    first, second = plane_groups()
    return [second + first]


def across_seg(array, by, swap):
    segs, ops = lax.axis_size("seg"), lax.axis_size("op")
    pairs = []
    for seg in range(segs):
        for op in range(ops):
            other = op ^ 2 if swap and not 0 <= seg + by < segs else op
            pairs.append((seg * ops + op, (seg + by) % segs * ops + other))
    return lax.ppermute(array, ("seg", "op"), pairs)


def sum_over_op(part):
    chunks = part.reshape(8, 128, 256)
    chunks = lax.all_to_all(chunks, "op", 0, 0, axis_index_groups=plane_groups(), tiled=True)
    (own,) = call(
        sum_kernel, (chunks,), [VMEM], [((128, 256), bf16)], [VMEM], flops=1_000_000, moved=600_000
    )
    other = lax.ppermute(own, "op", [(i, i ^ 2) for i in range(16)])
    both = (own.astype(f32) + other.astype(f32)).astype(bf16)
    spread = jnp.broadcast_to(both[None], (8, 128, 256))
    whole = lax.all_to_all(spread, "op", 0, 0, axis_index_groups=plane_groups(), tiled=True)
    return whole.reshape(4, 256, 256)


def shards(
    left_part, right_part, inverse_values, left_env, right_env, source, term_active, sketch, kept
):
    lenv, renv = left_env[0], right_env[0]
    slots, sectors = lenv.shape[:2]
    whole, cols = (sectors, 256, 256), sketch.shape[2]
    neighbour = across_seg(right_part, -1, False)[0]
    scaled, tests, lenv_near, renv_near = call(
        prepare_kernel,
        (left_part[0], inverse_values[0], sketch[0], lenv, renv),
        [VMEM] * 3 + [HBM] * 2,
        [(whole, bf16), ((cols, 256), f32), (lenv.shape, bf16), ((sectors, slots * 256, 256), bf16)],
        [VMEM] * 4,
        [pltpu.SemaphoreType.DMA((slots, 2))],
        moved=8_000_000,
    )
    inner = pltpu.VMEM((sectors, 256, slots * 256), bf16)
    first, part, ray = call(
        first_kernel,
        (source, term_active, scaled, neighbour, lenv_near, renv_near),
        [SMEM, SMEM] + [VMEM] * 4,
        [(whole, f32), (whole, bf16), ((8, 128), f32)],
        [HBM, VMEM, VMEM],
        [
            pltpu.VMEM(whole, f32), inner, pltpu.VMEM(whole, bf16), pltpu.VMEM(whole, f32),
            pltpu.SemaphoreType.DMA((sectors,)),
        ],
        flops=940_000_000, moved=6_000_000,
    )
    resid = sum_over_op(part)
    rays, coupling = call(
        second_kernel,
        (source, term_active, resid, ray, lenv, renv),
        [SMEM, SMEM] + [VMEM] * 4,
        [((16, 128), f32), ((8, 128), f32)],
        [VMEM] * 2,
        [inner],
        flops=800_000_000, moved=4_000_000,
    )
    rays = lax.all_to_all(rays, "op", 0, 0, axis_index_groups=upper_half_first(), tiled=True)
    right, right_low, image = call(
        truncate_kernel,
        (kept, rays, coupling, first, resid, tests),
        [SMEM] + [VMEM] * 5,
        [((sectors, cols, 256), f32), ((sectors, cols, 256), bf16), ((sectors, cols, 256), f32)],
        [VMEM] * 3,
        flops=1_200_000_000, moved=4_000_000,
    )
    handed = across_seg(right_low[None], 1, True)
    kept_state = jnp.einsum("bki,bkj->bij", image, right, precision=HIGHEST) / 256
    return (kept_state.astype(bf16)[None], handed)


def solution(mesh):
    placed = (
        P("seg", None, None, None),
        P("seg", None, None, None),
        P("seg", None, None),
        P("seg", "op", None, None, None),
        P("seg", "op", None, None, None),
        P("op", None),
        P("op"),
        P("seg", None, None),
        P("seg", None),
    )
    return jax.shard_map(
        shards,
        mesh=mesh,
        in_specs=placed,
        out_specs=(P("seg", None, None, None), P("seg", None, None, None)),
        check_vma=False,
    )
```

```python
import jax
import jax.numpy as jnp
from jax import lax
from jax.experimental import pallas as pl
from jax.experimental.pallas import tpu as pltpu
from jax.sharding import PartitionSpec as P

bf16, f32 = jnp.bfloat16, jnp.float32
HIGHEST = lax.Precision.HIGHEST
NN = (((1,), (0,)), ((), ()))
NT = (((1,), (1,)), ((), ()))
AHEAD = 2

SMEM = pl.BlockSpec(memory_space=pltpu.SMEM)
VMEM = pl.BlockSpec(memory_space=pltpu.VMEM)
HBM = pl.BlockSpec(memory_space=pltpu.HBM)


def call(kernel, operands, in_specs, outs, out_specs, scratch=(), flops=0, moved=0, vmem=24):
    return pl.pallas_call(
        kernel,
        out_shape=tuple(jax.ShapeDtypeStruct(shape, dtype) for shape, dtype in outs),
        in_specs=in_specs,
        out_specs=tuple(out_specs),
        scratch_shapes=list(scratch),
        compiler_params=pltpu.CompilerParams(vmem_limit_bytes=vmem * 2**20),
        cost_estimate=pl.CostEstimate(flops=flops, bytes_accessed=moved, transcendentals=0),
    )(*operands)


def prepare_kernel(left_part, inverse, lenv_hbm, renv_hbm, scaled, lenv, renv, sems):
    copies = []
    for slot in range(lenv.shape[0]):
        rows = pl.ds(slot * 256, 256)
        copies.append(pltpu.make_async_copy(lenv_hbm.at[slot], lenv.at[slot], sems.at[slot, 0]))
        copies.append(
            pltpu.make_async_copy(renv_hbm.at[slot], renv.at[:, rows, :], sems.at[slot, 1])
        )
    for copy in copies:
        copy.start()
    for b in range(left_part.shape[0]):
        scaled[b] = (left_part[b].astype(f32) * inverse[b : b + 1, :]).astype(bf16)
    for copy in copies:
        copy.wait()


def transpose_kernel(array, turned):
    turned[...] = array[...].T


def first_kernel(
    core, source, active, scaled, own_half, other_half, lenv, renv,
    first_hbm, part, ray, first, inner, vector, image, sems,
):
    slots, sectors = lenv.shape[:2]
    count = sectors * 256 * 256
    squares = jnp.zeros((1, 256), f32)
    half = sectors // 2
    for i in range(sectors):
        b = (half * core[0] + i) % sectors
        neighbour = own_half[i] if i < half else other_half[i - half]
        center = jnp.dot(scaled[b], neighbour, preferred_element_type=f32)
        image[b] = center
        squares += jnp.sum(center * center, axis=0, keepdims=True)
    scale = lax.rsqrt(jnp.sum(squares, axis=1, keepdims=True) / count + 1e-06)
    out_copies = []
    for b in range(sectors):
        scaled_center = image[b] * scale
        first[b] = scaled_center
        out_copies.append(pltpu.make_async_copy(first.at[b], first_hbm.at[b], sems.at[b]))
        out_copies[b].start()
        vector[b] = scaled_center.astype(bf16)
    for slot in range(slots):
        flag = active[slot].astype(f32)
        for b in range(sectors):
            product = jnp.dot(
                lenv[slot, b], vector[source[slot, b]], preferred_element_type=f32
            )
            inner[b, :, slot * 256 : (slot + 1) * 256] = (product * flag).astype(bf16)
    dots = jnp.zeros((1, 256), f32)
    for b in range(sectors):
        own = jnp.dot(inner[b], renv[b], preferred_element_type=f32)
        image[b] = own
        dots += jnp.sum(first[b] * own, axis=0, keepdims=True)
    own_ray = jnp.sum(dots, axis=1, keepdims=True) / count
    for b in range(sectors):
        part[b] = (image[b] - own_ray * first[b]).astype(bf16)
    ray[...] = jnp.broadcast_to(own_ray, ray.shape)
    for copy in out_copies:
        copy.wait()


def sum_kernel(chunks, total):
    summed = chunks[0].astype(f32)
    for i in range(1, chunks.shape[0]):
        summed += chunks[i].astype(f32)
    total[...] = summed.astype(bf16)


def second_kernel(source, active, resid, first_ray, lenv, renv, rays, coupling, inner):
    slots, sectors = lenv.shape[:2]
    count = sectors * 256 * 256
    for slot in range(slots):
        flag = active[slot].astype(f32)
        for b in range(sectors):
            product = jnp.dot(
                lenv[slot, b], resid[source[slot, b]], preferred_element_type=f32
            )
            inner[b, :, slot * 256 : (slot + 1) * 256] = (product * flag).astype(bf16)
    dots, squares = jnp.zeros((1, 256), f32), jnp.zeros((1, 256), f32)
    for b in range(sectors):
        below = jnp.concatenate([renv[slot, b] for slot in range(slots)], axis=0)
        own = jnp.dot(inner[b], below, preferred_element_type=f32)
        piece = resid[b].astype(f32)
        dots += jnp.sum(piece * own, axis=0, keepdims=True)
        squares += jnp.sum(piece * piece, axis=0, keepdims=True)
    mean_square = jnp.sum(squares, axis=1, keepdims=True) / count + 1e-06
    own_ray = jnp.sum(dots, axis=1, keepdims=True) / count / mean_square
    lane = lax.broadcasted_iota(jnp.int32, rays.shape, 1)
    rays[...] = jnp.where(lane == 0, first_ray[0:1, :], jnp.broadcast_to(own_ray, rays.shape))
    coupling[...] = jnp.broadcast_to(jnp.sqrt(mean_square), coupling.shape)


def split(array):
    high = array.astype(bf16)
    return high, (array - high.astype(f32)).astype(bf16)


def dot(left, right, dims=NN):
    return lax.dot_general(left, right, dims, preferred_element_type=f32)


def fine_dot(left, right, dims=NN):
    return dot(left[0], right[0], dims) + (
        dot(left[0], right[1], dims) + dot(left[1], right[0], dims)
    )


def invert_blocks(packed):
    size = packed.shape[0]
    row = lax.broadcasted_iota(jnp.int32, packed.shape, 0)
    lane = lax.broadcasted_iota(jnp.int32, packed.shape, 1)
    place = lane % size
    start = lane - place
    spot = place[0:1, :]

    def column(array, k):
        return jnp.take_along_axis(array, start + k, axis=1)

    queue = [(column(packed, k), column(packed, k + 1)) for k in range(0, 2 * AHEAD, 2)]
    for k in range(0, size, 2):
        left, right = queue.pop(0)
        if k + 2 * AHEAD < size:
            queue.append((column(packed, k + 2 * AHEAD), column(packed, k + 2 * AHEAD + 1)))
        top, cross, low = left[k : k + 1, :], left[k + 1 : k + 2, :], right[k + 1 : k + 2, :]
        scale = 1.0 / (top * low - cross * cross)

        def eliminate(old, upper, lower):
            upper, lower = low * upper - cross * lower, top * lower - cross * upper
            new = old - (left * upper + right * lower) * scale
            return jnp.where(
                row == k, upper * scale, jnp.where(row == k + 1, lower * scale, new)
            )

        upper = jnp.where(spot == k, 1.0, jnp.where(spot == k + 1, 0.0, packed[k : k + 1, :]))
        lower = jnp.where(spot == k, 0.0, jnp.where(spot == k + 1, 1.0, packed[k + 1 : k + 2, :]))
        rest = jnp.where((place == k) | (place == k + 1), 0.0, packed)
        packed = eliminate(rest, upper, lower)
        for i, pair in enumerate(queue):
            j = k + 2 * i + 2
            queue[i] = tuple(
                eliminate(old, left[n : n + 1, :], right[n : n + 1, :])
                for old, n in zip(pair, (j, j + 1), strict=True)
            )
    return packed


def invert(gram):
    sectors, cols, size = len(gram), gram[0].shape[0], 32
    row = lax.broadcasted_iota(jnp.int32, (cols, cols), 0)
    lane = lax.broadcasted_iota(jnp.int32, (cols, cols), 1)
    same = (row // size) == (lane // size)
    unit = jnp.where(row % size == lane % size, 1.0, 0.0).astype(f32)
    block_lane = lax.broadcasted_iota(jnp.int32, (size, cols), 1) // size
    for p in range(cols // size):
        rows = slice(p * size, (p + 1) * size)
        packed = jnp.zeros((size, cols), f32)
        for s in range(sectors):
            shift = ((s - p) * size) % cols
            turned = pltpu.roll(gram[s][rows], shift, 1) if shift else gram[s][rows]
            packed = jnp.where(block_lane == s, turned, packed)
        inverse = invert_blocks(packed)
        inverse = jnp.where(same, jnp.concatenate([inverse] * sectors, axis=0), 0.0)
        stacked = jnp.concatenate([g[rows] for g in gram], axis=0)
        stacked = jnp.where(lane // size == p, unit, stacked)
        panel = fine_dot(split(inverse), split(stacked))
        for s in range(sectors):
            own = panel[s * size : (s + 1) * size]
            tiled = jnp.concatenate([own] * (cols // size), axis=0)
            factor = jnp.where((lane // size == p) & (row // size != p), gram[s], 0.0)
            rest = jnp.where(lane // size == p, 0.0, gram[s])
            rest = jnp.where(row // size == p, tiled, rest)
            gram[s] = rest - fine_dot(split(factor), split(tiled))
    return gram


def truncate_kernel(kept, rays, coupling, first, resid, sketch, right, right_low, image):
    sectors, size = first.shape[:2]
    cols = sketch.shape[0]
    sums = jnp.sum(rays[...], axis=0, keepdims=True)
    ray_first, ray_second = sums[:, 0:1], sums[:, 1:2]
    between = coupling[0:1, 0:1]
    half = 0.5 * (ray_second - ray_first)
    weight = half + jnp.sqrt(half * half + between * between)
    length = lax.rsqrt(weight * weight + between * between)
    of_first, of_resid = weight * length, length
    tests = split(sketch[...])
    row = lax.broadcasted_iota(jnp.int32, (cols, cols), 0)
    lane = lax.broadcasted_iota(jnp.int32, (cols, cols), 1)
    wide_row = lax.broadcasted_iota(jnp.int32, (cols, size), 0)
    gram, correlation = [], []
    for b in range(sectors):
        ground = split(of_first * first[b] - of_resid * resid[b].astype(f32))
        own = jnp.where(wide_row < kept[0, b], fine_dot(tests, ground, NT), 0.0)
        image[b] = own
        own = split(own)
        empty = jnp.where((row == lane) & (row >= kept[0, b]), 1.0, 0.0)
        gram.append(fine_dot(own, own, NT) * (1.0 / (size * size)) + empty)
        correlation.append(fine_dot(own, ground))
    gram = invert(gram)
    for b in range(sectors):
        own = fine_dot(split(gram[b]), split(correlation[b])) * (1.0 / size)
        right[b] = own
        right_low[b] = own.astype(bf16)


def plane_groups():
    return [[x * 4 + z * 2 + c for x in range(4) for c in range(2)] for z in range(2)]


def upper_half_first():
    first, second = plane_groups()
    return [second + first]


def from_seg(array, by):
    size = lax.axis_size("seg")
    return lax.ppermute(array, "seg", [(i, (i + by) % size) for i in range(size)])


def sum_over_op(part, sketch):
    chunks = part.reshape(8, 128, 256)
    chunks = lax.all_to_all(chunks, "op", 0, 0, axis_index_groups=plane_groups(), tiled=True)
    (own,) = call(
        sum_kernel, (chunks,), [VMEM], [((128, 256), bf16)], [VMEM], flops=1_000_000, moved=600_000
    )
    other = lax.ppermute(own, "op", [(i, i ^ 2) for i in range(16)])
    (turned,) = call(transpose_kernel, (sketch,), [VMEM], [(sketch.shape[::-1], f32)], [VMEM])
    own, turned = lax.optimization_barrier((own, turned))
    both = (own.astype(f32) + other.astype(f32)).astype(bf16)
    spread = jnp.broadcast_to(both[None], (8, 128, 256))
    whole = lax.all_to_all(spread, "op", 0, 0, axis_index_groups=plane_groups(), tiled=True)
    return whole.reshape(4, 256, 256), turned


def shards(
    left_part, right_part, inverse_values, left_env, right_env, source, term_active, sketch, kept
):
    lenv, renv = left_env[0], right_env[0]
    slots, sectors = lenv.shape[:2]
    whole, cols = (sectors, 256, 256), sketch.shape[2]
    core = lax.axis_index("op") % 2
    half = sectors // 2
    own_half = lax.dynamic_slice_in_dim(right_part[0], half * core, half, 0)
    own_half = from_seg(own_half, -1)
    scaled, lenv_near, renv_near = call(
        prepare_kernel,
        (left_part[0], inverse_values[0], lenv, renv),
        [VMEM] * 2 + [HBM] * 2,
        [(whole, bf16), (lenv.shape, bf16), ((sectors, slots * 256, 256), bf16)],
        [VMEM] * 3,
        [pltpu.SemaphoreType.DMA((slots, 2))],
        moved=8_000_000,
    )
    inner = pltpu.VMEM((sectors, 256, slots * 256), bf16)
    own_half, scaled = lax.optimization_barrier((own_half, scaled))
    other_half = lax.ppermute(own_half, "op", [(i, i ^ 1) for i in range(lax.axis_size("op"))])
    core = core.astype(jnp.int32).reshape(1)
    first, part, ray = call(
        first_kernel,
        (core, source, term_active, scaled, own_half, other_half, lenv_near, renv_near),
        [SMEM] * 3 + [VMEM] * 5,
        [(whole, f32), (whole, bf16), ((8, 128), f32)],
        [HBM, VMEM, VMEM],
        [
            pltpu.VMEM(whole, f32), inner, pltpu.VMEM(whole, bf16), pltpu.VMEM(whole, f32),
            pltpu.SemaphoreType.DMA((sectors,)),
        ],
        flops=940_000_000, moved=6_000_000,
    )
    resid, tests = sum_over_op(part, sketch[0])
    rays, coupling = call(
        second_kernel,
        (source, term_active, resid, ray, lenv, renv),
        [SMEM, SMEM] + [VMEM] * 4,
        [((16, 128), f32), ((8, 128), f32)],
        [VMEM] * 2,
        [inner],
        flops=800_000_000, moved=4_000_000,
    )
    rays = lax.all_to_all(rays, "op", 0, 0, axis_index_groups=upper_half_first(), tiled=True)
    right, right_low, image = call(
        truncate_kernel,
        (kept, rays, coupling, first, resid, tests),
        [SMEM] + [VMEM] * 5,
        [((sectors, cols, 256), f32), ((sectors, cols, 256), bf16), ((sectors, cols, 256), f32)],
        [VMEM] * 3,
        flops=1_200_000_000, moved=4_000_000,
    )
    handed = from_seg(right_low, 1)
    kept_state = jnp.einsum("bki,bkj->bij", image, right, precision=HIGHEST) / 256
    return (kept_state.astype(bf16)[None], handed[None])


def solution(mesh):
    placed = (
        P("seg", None, None, None),
        P("seg", None, None, None),
        P("seg", None, None),
        P("seg", "op", None, None, None),
        P("seg", "op", None, None, None),
        P("op", None),
        P("op"),
        P("seg", None, None),
        P("seg", None),
    )
    return jax.shard_map(
        shards,
        mesh=mesh,
        in_specs=placed,
        out_specs=(P("seg", None, None, None), P("seg", None, None, None)),
        check_vma=False,
    )
```

```python
import jax
import jax.numpy as jnp
from jax import lax
from jax.experimental import pallas as pl
from jax.experimental.pallas import tpu as pltpu
from jax.sharding import PartitionSpec as P

bf16, f32 = jnp.bfloat16, jnp.float32
HIGHEST = lax.Precision.HIGHEST
NN = (((1,), (0,)), ((), ()))
NT = (((1,), (1,)), ((), ()))
AHEAD = 2

SMEM = pl.BlockSpec(memory_space=pltpu.SMEM)
VMEM = pl.BlockSpec(memory_space=pltpu.VMEM)
HBM = pl.BlockSpec(memory_space=pltpu.HBM)


def call(kernel, operands, in_specs, outs, out_specs, scratch=(), flops=0, moved=0, vmem=24):
    return pl.pallas_call(
        kernel,
        out_shape=tuple(jax.ShapeDtypeStruct(shape, dtype) for shape, dtype in outs),
        in_specs=in_specs,
        out_specs=tuple(out_specs),
        scratch_shapes=list(scratch),
        compiler_params=pltpu.CompilerParams(vmem_limit_bytes=vmem * 2**20),
        cost_estimate=pl.CostEstimate(flops=flops, bytes_accessed=moved, transcendentals=0),
    )(*operands)


def prepare_kernel(left_part, inverse, lenv_hbm, renv_hbm, scaled, lenv, renv, sems):
    copies = []
    for slot in range(lenv.shape[0]):
        rows = pl.ds(slot * 256, 256)
        copies.append(pltpu.make_async_copy(lenv_hbm.at[slot], lenv.at[slot], sems.at[slot, 0]))
        copies.append(
            pltpu.make_async_copy(renv_hbm.at[slot], renv.at[:, rows, :], sems.at[slot, 1])
        )
    for copy in copies:
        copy.start()
    for b in range(left_part.shape[0]):
        scaled[b] = (left_part[b].astype(f32) * inverse[b : b + 1, :]).astype(bf16)
    for copy in copies:
        copy.wait()


def transpose_kernel(array, turned):
    turned[...] = array[...].T


def first_kernel(
    core, source, active, scaled, own_half, other_half, lenv, renv,
    first_hbm, part, ray, first, inner, vector, image, sems,
):
    slots, sectors = lenv.shape[:2]
    count = sectors * 256 * 256
    squares = jnp.zeros((1, 256), f32)
    half = sectors // 2
    for i in range(sectors):
        b = (half * core[0] + i) % sectors
        neighbour = own_half[i] if i < half else other_half[i - half]
        center = jnp.dot(scaled[b], neighbour, preferred_element_type=f32)
        image[b] = center
        squares += jnp.sum(center * center, axis=0, keepdims=True)
    scale = lax.rsqrt(jnp.sum(squares, axis=1, keepdims=True) / count + 1e-06)
    out_copies = []
    for b in range(sectors):
        scaled_center = image[b] * scale
        first[b] = scaled_center
        out_copies.append(pltpu.make_async_copy(first.at[b], first_hbm.at[b], sems.at[b]))
        out_copies[b].start()
        vector[b] = scaled_center.astype(bf16)
    for slot in range(slots):
        flag = active[slot].astype(f32)
        for b in range(sectors):
            product = jnp.dot(
                lenv[slot, b], vector[source[slot, b]], preferred_element_type=f32
            )
            inner[b, :, slot * 256 : (slot + 1) * 256] = (product * flag).astype(bf16)
    dots = jnp.zeros((1, 256), f32)
    for b in range(sectors):
        own = jnp.dot(inner[b], renv[b], preferred_element_type=f32)
        image[b] = own
        dots += jnp.sum(first[b] * own, axis=0, keepdims=True)
    own_ray = jnp.sum(dots, axis=1, keepdims=True) / count
    for b in range(sectors):
        part[b] = (image[b] - own_ray * first[b]).astype(bf16)
    ray[...] = jnp.broadcast_to(own_ray, ray.shape)
    for copy in out_copies:
        copy.wait()


def sum_kernel(chunks, total):
    summed = chunks[0].astype(f32)
    for i in range(1, chunks.shape[0]):
        summed += chunks[i].astype(f32)
    total[...] = summed.astype(bf16)


def second_kernel(source, active, resid, first_ray, lenv, renv, rays, coupling, inner):
    slots, sectors = lenv.shape[:2]
    count = sectors * 256 * 256
    for slot in range(slots):
        flag = active[slot].astype(f32)
        for b in range(sectors):
            product = jnp.dot(
                lenv[slot, b], resid[source[slot, b]], preferred_element_type=f32
            )
            inner[b, :, slot * 256 : (slot + 1) * 256] = (product * flag).astype(bf16)
    dots, squares = jnp.zeros((1, 256), f32), jnp.zeros((1, 256), f32)
    for b in range(sectors):
        own = jnp.dot(inner[b], renv[b], preferred_element_type=f32)
        piece = resid[b].astype(f32)
        dots += jnp.sum(piece * own, axis=0, keepdims=True)
        squares += jnp.sum(piece * piece, axis=0, keepdims=True)
    mean_square = jnp.sum(squares, axis=1, keepdims=True) / count + 1e-06
    own_ray = jnp.sum(dots, axis=1, keepdims=True) / count / mean_square
    lane = lax.broadcasted_iota(jnp.int32, rays.shape, 1)
    rays[...] = jnp.where(lane == 0, first_ray[0:1, :], jnp.broadcast_to(own_ray, rays.shape))
    coupling[...] = jnp.broadcast_to(jnp.sqrt(mean_square), coupling.shape)


def split(array):
    high = array.astype(bf16)
    return high, (array - high.astype(f32)).astype(bf16)


def dot(left, right, dims=NN):
    return lax.dot_general(left, right, dims, preferred_element_type=f32)


def fine_dot(left, right, dims=NN):
    return dot(left[0], right[0], dims) + (
        dot(left[0], right[1], dims) + dot(left[1], right[0], dims)
    )


def invert_blocks(packed):
    size, lanes = packed.shape
    tiles = range(size // 8)
    row = lax.broadcasted_iota(jnp.int32, (8, lanes), 0)
    lane = lax.broadcasted_iota(jnp.int32, (8, lanes), 1)
    place = lane % size
    start = lane - place
    packed = [packed[8 * t : 8 * t + 8] for t in tiles]

    def column(k):
        return [jnp.take_along_axis(packed[t], start + k, axis=1) for t in tiles]

    def at(array, k):
        return array[k // 8][k % 8 : k % 8 + 1, :]

    queue = [(column(k), column(k + 1)) for k in range(0, 2 * AHEAD, 2)]
    for k in range(0, size, 2):
        left, right = queue.pop(0)
        if k + 2 * AHEAD < size:
            queue.append((column(k + 2 * AHEAD), column(k + 2 * AHEAD + 1)))
        top, cross, low = at(left, k), at(left, k + 1), at(right, k + 1)
        scale = 1.0 / (top * low - cross * cross)

        def eliminate(old, upper, lower):
            upper, lower = low * upper - cross * lower, top * lower - cross * upper
            new = [old[t] - (left[t] * upper + right[t] * lower) * scale for t in tiles]
            own = jnp.where(row == k % 8, upper * scale, lower * scale)
            new[k // 8] = jnp.where((row == k % 8) | (row == k % 8 + 1), own, new[k // 8])
            return new

        first, second = place == k, place == k + 1
        upper = jnp.where(first[0:1], 1.0, jnp.where(second[0:1], 0.0, at(packed, k)))
        lower = jnp.where(first[0:1], 0.0, jnp.where(second[0:1], 1.0, at(packed, k + 1)))
        packed = eliminate(
            [jnp.where(first | second, 0.0, packed[t]) for t in tiles], upper, lower
        )
        for i, pair in enumerate(queue):
            j = k + 2 * i + 2
            queue[i] = tuple(
                eliminate(old, at(left, n), at(right, n))
                for old, n in zip(pair, (j, j + 1), strict=True)
            )
    return jnp.concatenate(packed, axis=0)


def invert(gram):
    sectors, cols, size = len(gram), gram[0].shape[0], 32
    row = lax.broadcasted_iota(jnp.int32, (cols, cols), 0)
    lane = lax.broadcasted_iota(jnp.int32, (cols, cols), 1)
    same = (row // size) == (lane // size)
    unit = jnp.where(row % size == lane % size, 1.0, 0.0).astype(f32)
    block_lane = lax.broadcasted_iota(jnp.int32, (size, cols), 1) // size
    for p in range(cols // size):
        rows = slice(p * size, (p + 1) * size)
        packed = jnp.zeros((size, cols), f32)
        for s in range(sectors):
            shift = ((s - p) * size) % cols
            turned = pltpu.roll(gram[s][rows], shift, 1) if shift else gram[s][rows]
            packed = jnp.where(block_lane == s, turned, packed)
        inverse = invert_blocks(packed)
        inverse = jnp.where(same, jnp.concatenate([inverse] * sectors, axis=0), 0.0)
        stacked = jnp.concatenate([g[rows] for g in gram], axis=0)
        stacked = jnp.where(lane // size == p, unit, stacked)
        panel = fine_dot(split(inverse), split(stacked))
        for s in range(sectors):
            own = panel[s * size : (s + 1) * size]
            tiled = jnp.concatenate([own] * (cols // size), axis=0)
            factor = jnp.where((lane // size == p) & (row // size != p), gram[s], 0.0)
            rest = jnp.where(lane // size == p, 0.0, gram[s])
            rest = jnp.where(row // size == p, tiled, rest)
            gram[s] = rest - fine_dot(split(factor), split(tiled))
    return gram


def truncate_kernel(kept, rays, coupling, first, resid, sketch, right, right_low, image):
    sectors, size = first.shape[:2]
    cols = sketch.shape[0]
    sums = jnp.sum(rays[...], axis=0, keepdims=True)
    ray_first, ray_second = sums[:, 0:1], sums[:, 1:2]
    between = coupling[0:1, 0:1]
    half = 0.5 * (ray_second - ray_first)
    weight = half + jnp.sqrt(half * half + between * between)
    length = lax.rsqrt(weight * weight + between * between)
    of_first, of_resid = weight * length, length
    tests = split(sketch[...])
    row = lax.broadcasted_iota(jnp.int32, (cols, cols), 0)
    lane = lax.broadcasted_iota(jnp.int32, (cols, cols), 1)
    wide_row = lax.broadcasted_iota(jnp.int32, (cols, size), 0)
    gram, correlation = [], []
    for b in range(sectors):
        ground = split(of_first * first[b] - of_resid * resid[b].astype(f32))
        own = jnp.where(wide_row < kept[0, b], fine_dot(tests, ground, NT), 0.0)
        image[b] = own
        own = split(own)
        empty = jnp.where((row == lane) & (row >= kept[0, b]), 1.0, 0.0)
        gram.append(fine_dot(own, own, NT) * (1.0 / (size * size)) + empty)
        correlation.append(fine_dot(own, ground))
    gram = invert(gram)
    for b in range(sectors):
        own = fine_dot(split(gram[b]), split(correlation[b])) * (1.0 / size)
        right[b] = own
        right_low[b] = own.astype(bf16)


def plane_groups():
    return [[x * 4 + z * 2 + c for x in (2, 1, 3, 0) for c in (1, 0)] for z in range(2)]


def upper_half_first():
    lower, upper = plane_groups()
    return [upper + lower]


def from_seg(array, by):
    size = lax.axis_size("seg")
    return lax.ppermute(array, "seg", [(i, (i + by) % size) for i in range(size)])


def sum_over_op(part, sketch):
    chunks = part.reshape(8, 128, 256)
    chunks = lax.all_to_all(chunks, "op", 0, 0, axis_index_groups=plane_groups(), tiled=True)
    (own,) = call(
        sum_kernel, (chunks,), [VMEM], [((128, 256), bf16)], [VMEM], flops=1_000_000, moved=600_000
    )
    other = lax.ppermute(own, "op", [(i, i ^ 2) for i in range(16)])
    (turned,) = call(transpose_kernel, (sketch,), [VMEM], [(sketch.shape[::-1], f32)], [VMEM])
    own, turned = lax.optimization_barrier((own, turned))
    both = (own.astype(f32) + other.astype(f32)).astype(bf16)
    spread = jnp.broadcast_to(both[None], (8, 128, 256))
    whole = lax.all_to_all(spread, "op", 0, 0, axis_index_groups=plane_groups(), tiled=True)
    return whole.reshape(4, 256, 256), turned


def shards(
    left_part, right_part, inverse_values, left_env, right_env, source, term_active, sketch, kept
):
    lenv, renv = left_env[0], right_env[0]
    slots, sectors = lenv.shape[:2]
    whole, cols = (sectors, 256, 256), sketch.shape[2]
    core = lax.axis_index("op") % 2
    half = sectors // 2
    own_half = lax.dynamic_slice_in_dim(right_part[0], half * core, half, 0)
    own_half = from_seg(own_half, -1)
    scaled, lenv_near, renv_near = call(
        prepare_kernel,
        (left_part[0], inverse_values[0], lenv, renv),
        [VMEM] * 2 + [HBM] * 2,
        [(whole, bf16), (lenv.shape, bf16), ((sectors, slots * 256, 256), bf16)],
        [VMEM] * 3,
        [pltpu.SemaphoreType.DMA((slots, 2))],
        moved=8_000_000,
    )
    inner = pltpu.VMEM((sectors, 256, slots * 256), bf16)
    own_half, scaled = lax.optimization_barrier((own_half, scaled))
    other_half = lax.ppermute(own_half, "op", [(i, i ^ 1) for i in range(lax.axis_size("op"))])
    core = core.astype(jnp.int32).reshape(1)
    first, part, ray = call(
        first_kernel,
        (core, source, term_active, scaled, own_half, other_half, lenv_near, renv_near),
        [SMEM] * 3 + [VMEM] * 5,
        [(whole, f32), (whole, bf16), ((8, 128), f32)],
        [HBM, VMEM, VMEM],
        [
            pltpu.VMEM(whole, f32), inner, pltpu.VMEM(whole, bf16), pltpu.VMEM(whole, f32),
            pltpu.SemaphoreType.DMA((sectors,)),
        ],
        flops=940_000_000, moved=6_000_000,
    )
    resid, tests = sum_over_op(part, sketch[0])
    rays, coupling = call(
        second_kernel,
        (source, term_active, resid, ray, lenv_near, renv_near),
        [SMEM, SMEM] + [VMEM] * 4,
        [((16, 128), f32), ((8, 128), f32)],
        [VMEM] * 2,
        [inner],
        flops=800_000_000, moved=4_000_000,
    )
    rays = lax.all_to_all(rays, "op", 0, 0, axis_index_groups=upper_half_first(), tiled=True)
    right, right_low, image = call(
        truncate_kernel,
        (kept, rays, coupling, first, resid, tests),
        [SMEM] + [VMEM] * 5,
        [((sectors, cols, 256), f32), ((sectors, cols, 256), bf16), ((sectors, cols, 256), f32)],
        [VMEM] * 3,
        flops=1_200_000_000, moved=4_000_000,
    )
    handed = from_seg(right_low, 1)
    kept_state = jnp.einsum("bki,bkj->bij", image, right, precision=HIGHEST) / 256
    return (kept_state.astype(bf16)[None], handed[None])


def solution(mesh):
    placed = (
        P("seg", None, None, None),
        P("seg", None, None, None),
        P("seg", None, None),
        P("seg", "op", None, None, None),
        P("seg", "op", None, None, None),
        P("op", None),
        P("op"),
        P("seg", None, None),
        P("seg", None),
    )
    return jax.shard_map(
        shards,
        mesh=mesh,
        in_specs=placed,
        out_specs=(P("seg", None, None, None), P("seg", None, None, None)),
        check_vma=False,
    )
```

```python
import jax
import jax.numpy as jnp
from jax import lax
from jax.experimental import pallas as pl
from jax.experimental.pallas import tpu as pltpu
from jax.sharding import PartitionSpec as P

bf16, f32 = jnp.bfloat16, jnp.float32
HIGHEST = lax.Precision.HIGHEST
NN = (((1,), (0,)), ((), ()))
NT = (((1,), (1,)), ((), ()))
AHEAD = 2

SMEM = pl.BlockSpec(memory_space=pltpu.SMEM)
VMEM = pl.BlockSpec(memory_space=pltpu.VMEM)
HBM = pl.BlockSpec(memory_space=pltpu.HBM)


def call(kernel, operands, in_specs, outs, out_specs, scratch=(), flops=0, moved=0, vmem=24):
    return pl.pallas_call(
        kernel,
        out_shape=tuple(jax.ShapeDtypeStruct(shape, dtype) for shape, dtype in outs),
        in_specs=in_specs,
        out_specs=tuple(out_specs),
        scratch_shapes=list(scratch),
        compiler_params=pltpu.CompilerParams(vmem_limit_bytes=vmem * 2**20),
        cost_estimate=pl.CostEstimate(flops=flops, bytes_accessed=moved, transcendentals=0),
    )(*operands)


def prepare_kernel(left_part, inverse, lenv_hbm, renv_hbm, scaled, lenv, renv, sems):
    copies = []
    for slot in range(lenv.shape[0]):
        rows = pl.ds(slot * 256, 256)
        copies.append(pltpu.make_async_copy(lenv_hbm.at[slot], lenv.at[slot], sems.at[slot, 0]))
        copies.append(
            pltpu.make_async_copy(renv_hbm.at[slot], renv.at[:, rows, :], sems.at[slot, 1])
        )
    for copy in copies:
        copy.start()
    for b in range(left_part.shape[0]):
        scaled[b] = (left_part[b].astype(f32) * inverse[b : b + 1, :]).astype(bf16)
    for copy in copies:
        copy.wait()


def transpose_kernel(array, turned):
    turned[...] = array[...].T


def center_kernel(core, scaled, neighbour, center, squares):
    half = neighbour.shape[0]
    total = jnp.zeros((1, 256), f32)
    for i in range(half):
        own = jnp.dot(scaled[half * core[0] + i], neighbour[i], preferred_element_type=f32)
        center[i] = own
        total += jnp.sum(own * own, axis=0, keepdims=True)
    squares[...] = jnp.broadcast_to(total, squares.shape)


def first_kernel(
    core, source, active, scaled, own_center, own_squares, other_half, lenv, renv,
    first, part, ray, inner, vector, image,
):
    slots, sectors = lenv.shape[:2]
    count = sectors * 256 * 256
    squares = own_squares[0:1, :]
    half = sectors // 2
    for i in range(half):
        image[half * core[0] + i] = own_center[i]
        b = half * (1 - core[0]) + i
        center = jnp.dot(scaled[b], other_half[i], preferred_element_type=f32)
        image[b] = center
        squares += jnp.sum(center * center, axis=0, keepdims=True)
    scale = lax.rsqrt(jnp.sum(squares, axis=1, keepdims=True) / count + 1e-06)
    for b in range(sectors):
        scaled_center = image[b] * scale
        first[b] = scaled_center
        vector[b] = scaled_center.astype(bf16)
    for slot in range(slots):
        flag = active[slot].astype(f32)
        for b in range(sectors):
            product = jnp.dot(
                lenv[slot, b], vector[source[slot, b]], preferred_element_type=f32
            )
            inner[b, :, slot * 256 : (slot + 1) * 256] = (product * flag).astype(bf16)
    dots = jnp.zeros((1, 256), f32)
    for b in range(sectors):
        own = jnp.dot(inner[b], renv[b], preferred_element_type=f32)
        image[b] = own
        dots += jnp.sum(first[b] * own, axis=0, keepdims=True)
    own_ray = jnp.sum(dots, axis=1, keepdims=True) / count
    for b in range(sectors):
        part[b] = (image[b] - own_ray * first[b]).astype(bf16)
    ray[...] = jnp.broadcast_to(own_ray, ray.shape)


def sum_kernel(chunks, total):
    summed = chunks[0].astype(f32)
    for i in range(1, chunks.shape[0]):
        summed += chunks[i].astype(f32)
    total[...] = summed.astype(bf16)


def second_kernel(source, active, resid, first_ray, lenv, renv, rays, coupling, inner):
    slots, sectors = lenv.shape[:2]
    count = sectors * 256 * 256
    for slot in range(slots):
        flag = active[slot].astype(f32)
        for b in range(sectors):
            product = jnp.dot(
                lenv[slot, b], resid[source[slot, b]], preferred_element_type=f32
            )
            inner[b, :, slot * 256 : (slot + 1) * 256] = (product * flag).astype(bf16)
    dots, squares = jnp.zeros((1, 256), f32), jnp.zeros((1, 256), f32)
    for b in range(sectors):
        own = jnp.dot(inner[b], renv[b], preferred_element_type=f32)
        piece = resid[b].astype(f32)
        dots += jnp.sum(piece * own, axis=0, keepdims=True)
        squares += jnp.sum(piece * piece, axis=0, keepdims=True)
    mean_square = jnp.sum(squares, axis=1, keepdims=True) / count + 1e-06
    own_ray = jnp.sum(dots, axis=1, keepdims=True) / count / mean_square
    lane = lax.broadcasted_iota(jnp.int32, rays.shape, 1)
    rays[...] = jnp.where(lane == 0, first_ray[0:1, :], jnp.broadcast_to(own_ray, rays.shape))
    coupling[...] = jnp.broadcast_to(jnp.sqrt(mean_square), coupling.shape)


def split(array):
    high = array.astype(bf16)
    return high, (array - high.astype(f32)).astype(bf16)


def dot(left, right, dims=NN):
    return lax.dot_general(left, right, dims, preferred_element_type=f32)


def fine_dot(left, right, dims=NN):
    return dot(left[0], right[0], dims) + (
        dot(left[0], right[1], dims) + dot(left[1], right[0], dims)
    )


def invert_blocks(packed):
    size, lanes = packed.shape
    tiles = range(size // 8)
    row = lax.broadcasted_iota(jnp.int32, (8, lanes), 0)
    lane = lax.broadcasted_iota(jnp.int32, (8, lanes), 1)
    place = lane % size
    start = lane - place
    packed = [packed[8 * t : 8 * t + 8] for t in tiles]

    def column(k):
        return [jnp.take_along_axis(packed[t], start + k, axis=1) for t in tiles]

    def at(array, k):
        return array[k // 8][k % 8 : k % 8 + 1, :]

    queue = [(column(k), column(k + 1)) for k in range(0, 2 * AHEAD, 2)]
    for k in range(0, size, 2):
        left, right = queue.pop(0)
        if k + 2 * AHEAD < size:
            queue.append((column(k + 2 * AHEAD), column(k + 2 * AHEAD + 1)))
        top, cross, low = at(left, k), at(left, k + 1), at(right, k + 1)
        scale = 1.0 / (top * low - cross * cross)

        def eliminate(old, upper, lower):
            upper, lower = low * upper - cross * lower, top * lower - cross * upper
            new = [old[t] - (left[t] * upper + right[t] * lower) * scale for t in tiles]
            own = jnp.where(row == k % 8, upper * scale, lower * scale)
            new[k // 8] = jnp.where((row == k % 8) | (row == k % 8 + 1), own, new[k // 8])
            return new

        first, second = place == k, place == k + 1
        upper = jnp.where(first[0:1], 1.0, jnp.where(second[0:1], 0.0, at(packed, k)))
        lower = jnp.where(first[0:1], 0.0, jnp.where(second[0:1], 1.0, at(packed, k + 1)))
        packed = eliminate(
            [jnp.where(first | second, 0.0, packed[t]) for t in tiles], upper, lower
        )
        for i, pair in enumerate(queue):
            j = k + 2 * i + 2
            queue[i] = tuple(
                eliminate(old, at(left, n), at(right, n))
                for old, n in zip(pair, (j, j + 1), strict=True)
            )
    return jnp.concatenate(packed, axis=0)


def invert(gram):
    sectors, cols, size = len(gram), gram[0].shape[0], 32
    row = lax.broadcasted_iota(jnp.int32, (cols, cols), 0)
    lane = lax.broadcasted_iota(jnp.int32, (cols, cols), 1)
    same = (row // size) == (lane // size)
    unit = jnp.where(row % size == lane % size, 1.0, 0.0).astype(f32)
    block_lane = lax.broadcasted_iota(jnp.int32, (size, cols), 1) // size
    for p in range(cols // size):
        rows = slice(p * size, (p + 1) * size)
        packed = jnp.zeros((size, cols), f32)
        for s in range(sectors):
            shift = ((s - p) * size) % cols
            turned = pltpu.roll(gram[s][rows], shift, 1) if shift else gram[s][rows]
            packed = jnp.where(block_lane == s, turned, packed)
        inverse = invert_blocks(packed)
        inverse = jnp.where(same, jnp.concatenate([inverse] * sectors, axis=0), 0.0)
        stacked = jnp.concatenate([g[rows] for g in gram], axis=0)
        stacked = jnp.where(lane // size == p, unit, stacked)
        panel = fine_dot(split(inverse), split(stacked))
        for s in range(sectors):
            own = panel[s * size : (s + 1) * size]
            tiled = jnp.concatenate([own] * (cols // size), axis=0)
            factor = jnp.where((lane // size == p) & (row // size != p), gram[s], 0.0)
            rest = jnp.where(lane // size == p, 0.0, gram[s])
            rest = jnp.where(row // size == p, tiled, rest)
            gram[s] = rest - fine_dot(split(factor), split(tiled))
    return gram


def truncate_kernel(kept, rays, coupling, first, resid, sketch, right, right_low, image):
    sectors, size = first.shape[:2]
    cols = sketch.shape[0]
    sums = jnp.sum(rays[...], axis=0, keepdims=True)
    ray_first, ray_second = sums[:, 0:1], sums[:, 1:2]
    between = coupling[0:1, 0:1]
    half = 0.5 * (ray_second - ray_first)
    weight = half + jnp.sqrt(half * half + between * between)
    length = lax.rsqrt(weight * weight + between * between)
    of_first, of_resid = weight * length, length
    tests = split(sketch[...])
    row = lax.broadcasted_iota(jnp.int32, (cols, cols), 0)
    lane = lax.broadcasted_iota(jnp.int32, (cols, cols), 1)
    wide_row = lax.broadcasted_iota(jnp.int32, (cols, size), 0)
    gram, correlation = [], []
    for b in range(sectors):
        ground = split(of_first * first[b] - of_resid * resid[b].astype(f32))
        own = jnp.where(wide_row < kept[0, b], fine_dot(tests, ground, NT), 0.0)
        image[b] = own
        own = split(own)
        empty = jnp.where((row == lane) & (row >= kept[0, b]), 1.0, 0.0)
        gram.append(fine_dot(own, own, NT) * (1.0 / (size * size)) + empty)
        correlation.append(fine_dot(own, ground))
    gram = invert(gram)
    for b in range(sectors):
        own = fine_dot(split(gram[b]), split(correlation[b])) * (1.0 / size)
        right[b] = own
        right_low[b] = own.astype(bf16)


def plane_groups():
    return [[x * 4 + z * 2 + c for x in (2, 1, 3, 0) for c in (1, 0)] for z in range(2)]


def upper_half_first():
    lower, upper = plane_groups()
    return [upper + lower]


def from_seg(array, by):
    size = lax.axis_size("seg")
    return lax.ppermute(array, "seg", [(i, (i + by) % size) for i in range(size)])


def sum_over_op(part, sketch):
    chunks = part.reshape(8, 128, 256)
    chunks = lax.all_to_all(chunks, "op", 0, 0, axis_index_groups=plane_groups(), tiled=True)
    (own,) = call(
        sum_kernel, (chunks,), [VMEM], [((128, 256), bf16)], [VMEM], flops=1_000_000, moved=600_000
    )
    other = lax.ppermute(own, "op", [(i, i ^ 2) for i in range(16)])
    (turned,) = call(transpose_kernel, (sketch,), [VMEM], [(sketch.shape[::-1], f32)], [VMEM])
    own, turned = lax.optimization_barrier((own, turned))
    both = (own.astype(f32) + other.astype(f32)).astype(bf16)
    spread = jnp.broadcast_to(both[None], (8, 128, 256))
    whole = lax.all_to_all(spread, "op", 0, 0, axis_index_groups=plane_groups(), tiled=True)
    return whole.reshape(4, 256, 256), turned


def shards(
    left_part, right_part, inverse_values, left_env, right_env, source, term_active, sketch, kept
):
    lenv, renv = left_env[0], right_env[0]
    slots, sectors = lenv.shape[:2]
    whole, cols = (sectors, 256, 256), sketch.shape[2]
    core = lax.axis_index("op") % 2
    half = sectors // 2
    own_half = lax.dynamic_slice_in_dim(right_part[0], half * core, half, 0)
    own_half = from_seg(own_half, -1)
    scaled, lenv_near, renv_near = call(
        prepare_kernel,
        (left_part[0], inverse_values[0], lenv, renv),
        [VMEM] * 2 + [HBM] * 2,
        [(whole, bf16), (lenv.shape, bf16), ((sectors, slots * 256, 256), bf16)],
        [VMEM] * 3,
        [pltpu.SemaphoreType.DMA((slots, 2))],
        moved=8_000_000,
    )
    inner = pltpu.VMEM((sectors, 256, slots * 256), bf16)
    own_half, scaled = lax.optimization_barrier((own_half, scaled))
    other_half = lax.ppermute(own_half, "op", [(i, i ^ 1) for i in range(lax.axis_size("op"))])
    core = core.astype(jnp.int32).reshape(1)
    own_center, own_squares = call(
        center_kernel, (core, scaled, own_half), [SMEM] + [VMEM] * 2,
        [((half, 256, 256), f32), ((8, 256), f32)], [VMEM] * 2,
        flops=900_000_000, moved=1_000_000,
    )
    first, part, ray = call(
        first_kernel,
        (core, source, term_active, scaled, own_center, own_squares, other_half, lenv_near, renv_near),
        [SMEM] * 3 + [VMEM] * 6,
        [(whole, f32), (whole, bf16), ((8, 128), f32)],
        [VMEM] * 3,
        [inner, pltpu.VMEM(whole, bf16), pltpu.VMEM(whole, f32)],
        flops=940_000_000, moved=6_000_000,
    )
    resid, tests = sum_over_op(part, sketch[0])
    rays, coupling = call(
        second_kernel,
        (source, term_active, resid, ray, lenv_near, renv_near),
        [SMEM, SMEM] + [VMEM] * 4,
        [((16, 128), f32), ((8, 128), f32)],
        [VMEM] * 2,
        [inner],
        flops=800_000_000, moved=4_000_000,
    )
    rays = lax.all_to_all(rays, "op", 0, 0, axis_index_groups=upper_half_first(), tiled=True)
    right, right_low, image = call(
        truncate_kernel,
        (kept, rays, coupling, first, resid, tests),
        [SMEM] + [VMEM] * 5,
        [((sectors, cols, 256), f32), ((sectors, cols, 256), bf16), ((sectors, cols, 256), f32)],
        [VMEM] * 3,
        flops=1_200_000_000, moved=4_000_000,
    )
    handed = from_seg(right_low, 1)
    kept_state = jnp.einsum("bki,bkj->bij", image, right, precision=HIGHEST) / 256
    return (kept_state.astype(bf16)[None], handed[None])


def solution(mesh):
    placed = (
        P("seg", None, None, None),
        P("seg", None, None, None),
        P("seg", None, None),
        P("seg", "op", None, None, None),
        P("seg", "op", None, None, None),
        P("op", None),
        P("op"),
        P("seg", None, None),
        P("seg", None),
    )
    return jax.shard_map(
        shards,
        mesh=mesh,
        in_specs=placed,
        out_specs=(P("seg", None, None, None), P("seg", None, None, None)),
        check_vma=False,
    )
```
